32 devices in a mesh: dp: 8 (over y, x, core), head: 4 (over z).
Axes of the slice: x: 2, y: 2, z: 4, core: 2. Of those that a mesh axis runs over, the one named last changes fastest.
Arguments:
- tokens: bfloat16 [2, 8, 1024, 1536], P(None, 'dp', 'head'), may hold values from -6 to 6
- lengths: int32 [2, 8], P(None, 'dp'), may hold values from 128 to 1024, as said below
- cotangent: bfloat16 [2, 8, 1024, 1536], P(None, 'dp', 'head'), may hold values from -6 to 6
- q_weight: bfloat16 [1536, 1536], P('dp', 'head'), may hold values from -0.15625 to 0.15625
- k_weight: bfloat16 [1536, 1536], P('dp', 'head'), may hold values from -0.15625 to 0.15625
- v_weight: bfloat16 [1536, 1536], P('dp', 'head'), may hold values from -0.15625 to 0.15625
- direction_weight: bfloat16 [1536, 1536], P('dp', 'head'), may hold values from -0.15625 to 0.15625
- beta_weight: bfloat16 [1536, 12], P('dp', 'head'), may hold values from -0.15625 to 0.15625
- out_weight: bfloat16 [1536, 1536], P('head', 'dp'), may hold values from -2.5 to 2.5
- gate_weight: bfloat16 [1536, 4096], P('dp', 'head'), may hold values from -0.15625 to 0.15625
- up_weight: bfloat16 [1536, 4096], P('dp', 'head'), may hold values from -0.15625 to 0.15625
- down_weight: bfloat16 [4096, 1536], P('head', 'dp'), may hold values from -0.09375 to 0.09375
- norm_gain_one: bfloat16 [1536], P('dp'), may hold values from 0.5 to 1.5
- norm_gain_two: bfloat16 [1536], P('dp'), may hold values from 0.5 to 1.5
Outputs:
- block_out: bfloat16 [2, 8, 1024, 1536], P(None, 'dp', 'head')
- input_grad: float32 [2, 8, 1024, 1536], P(None, 'dp', 'head')
- q_weight_grad: float32 [1536, 1536], P('dp', 'head')
- k_weight_grad: float32 [1536, 1536], P('dp', 'head')
- v_weight_grad: float32 [1536, 1536], P('dp', 'head')
- direction_weight_grad: float32 [1536, 1536], P('dp', 'head')
- beta_weight_grad: float32 [1536, 12], P('dp', 'head')
- out_weight_grad: float32 [1536, 1536], P('head', 'dp')
- gate_weight_grad: float32 [1536, 4096], P('dp', 'head')
- up_weight_grad: float32 [1536, 4096], P('dp', 'head')
- down_weight_grad: float32 [4096, 1536], P('head', 'dp')
- norm_gain_one_grad: float32 [1536], P('dp')
- norm_gain_two_grad: float32 [1536], P('dp')
The draws below stay inside these ranges and needn't reach their ends.
Inputs may be any that keep to these rules, and one draw needn't show every extreme that they name: `lengths`: within each aligned group of 1 slots, taken over all 2 micro-batches together, one slot is full (1024 valid tokens).
All inputs are finite; a program needn't handle non-finite values.
Results may differ from the reference program's by a relative error of at most 0.022.
Values may be sent and summed in bfloat16 or wider, within the bound.
No kernel may reach another device: no remote copies, remote signals or barrier semaphores. Data moves between devices by JAX's collectives and lax.ppermute only.
A program may use at most 448 MiB of HBM per device.

```python
import jax
import jax.numpy as jnp
from jax import lax

D = 1536
HEADS = 12
HEAD_DIM = 128
FF = 4096
SPAN = 64
LEN = 1024
MB = 2
SEQ_DEV = 1
SEQS = 8


def draw_lengths(key, part):
    key = jax.random.fold_in(key, 11)
    first_key, second_key = jax.random.split(key)
    drawn_lengths = jax.random.randint(first_key, (MB, SEQS), LEN // 8, LEN + 1, dtype=jnp.int32)
    groups = SEQS // SEQ_DEV
    picked = jax.random.randint(second_key, (groups,), 0, MB * SEQ_DEV, dtype=jnp.int32)
    slot_index = jnp.arange(SEQS, dtype=jnp.int32)
    micro_index = jnp.arange(MB, dtype=jnp.int32)
    local_slot = micro_index[:, None] * SEQ_DEV + slot_index[None, :] % SEQ_DEV
    chosen_slot = picked[slot_index // SEQ_DEV]
    return jnp.where(local_slot == chosen_slot[None, :], LEN, drawn_lengths).astype(jnp.int32)


def draw_cotangent(key, part):
    key = jax.random.fold_in(key, 23)
    first_key = jax.random.fold_in(key, 0)
    rising = 0.5 + jnp.arange(SEQS, dtype=jnp.float32) / max(SEQS - 1, 1)
    base_values = jax.random.truncated_normal(first_key, -4.0, 4.0, (MB, SEQS, LEN, D), jnp.float32)
    return (base_values * rising[None, :, None, None]).astype(jnp.bfloat16)


def block_scale(rng, extent, cuts, smallest, top_value):
    gain, own = 1.0, jax.random.fold_in(rng, 6)
    for dim, blocks in cuts:
        heights = jnp.exp(jax.random.uniform(jax.random.fold_in(own, dim), (blocks,), jnp.float32, smallest / len(cuts), top_value / len(cuts)))
        gain = gain * jnp.repeat(heights, extent[dim] // blocks).reshape([-1 if axis == dim else 1 for axis in range(len(extent))])
    return gain


def centred(rng, shape, spread, bound, cuts=(), kind=jnp.bfloat16):
    loudness = block_scale(rng, shape, cuts, -0.22, 0.18) if cuts else 1.0
    entries = jax.random.normal(rng, shape, jnp.float32) * spread * loudness
    return jnp.minimum(jnp.maximum(entries, -bound), bound).astype(kind)


def setup_inputs(seed: int = 0) -> dict:
    keys = jax.random.split(jax.random.key(seed), 15)
    tokens = centred(keys[0], (MB, SEQS, LEN, D), 1.0, 6.0, ((1, 8), (2, 4)))
    lengths = draw_lengths(jax.random.fold_in(keys[14], 71), 0)
    cotangent = draw_cotangent(jax.random.fold_in(keys[14], 71), 0)
    q_weight = centred(keys[3], (D, HEADS * HEAD_DIM), D ** -0.5, 0.15625, ((0, 8), (1, 4)))
    k_weight = centred(keys[4], (D, HEADS * HEAD_DIM), D ** -0.5, 0.15625, ((0, 8), (1, 4)))
    v_weight = centred(keys[5], (D, HEADS * HEAD_DIM), D ** -0.5, 0.15625, ((0, 8), (1, 4)))
    direction_weight = centred(keys[6], (D, HEADS * HEAD_DIM), D ** -0.5, 0.15625, ((0, 8), (1, 4)))
    beta_weight = centred(keys[7], (D, HEADS), D ** -0.5, 0.15625, ((0, 8), (1, 4)))
    out_weight = centred(keys[8], (HEADS * HEAD_DIM, D), (HEADS * HEAD_DIM * 4 // LEN) ** -0.5, 2.5, ((0, 4), (1, 8)))
    gate_weight = centred(keys[9], (D, FF), D ** -0.5, 0.15625, ((0, 8), (1, 4)))
    up_weight = centred(keys[10], (D, FF), D ** -0.5, 0.15625, ((0, 8), (1, 4)))
    down_weight = centred(keys[11], (FF, D), FF ** -0.5, 0.09375, ((0, 4), (1, 8)))
    norm_gain_one = jnp.clip(1.0 + 0.1 * jax.random.normal(keys[12], (D,), jnp.float32), 0.5, 1.5).astype(jnp.bfloat16)
    norm_gain_two = jnp.clip(1.0 + 0.1 * jax.random.normal(keys[13], (D,), jnp.float32), 0.5, 1.5).astype(jnp.bfloat16)
    return dict(tokens=tokens, lengths=lengths, cotangent=cotangent, q_weight=q_weight, k_weight=k_weight, v_weight=v_weight, direction_weight=direction_weight, beta_weight=beta_weight, out_weight=out_weight, gate_weight=gate_weight, up_weight=up_weight, down_weight=down_weight, norm_gain_one=norm_gain_one, norm_gain_two=norm_gain_two)


@jax.custom_vjp
def low(v):
    return lax.optimization_barrier(v.astype(jnp.bfloat16)).astype(jnp.float32)

@jax.custom_vjp
def low_back(v):
    return v

def low_keep(v):
    return (low(v), None)

def low_pass(kept, grad):
    return (grad,)

def back_keep(v):
    return (v, None)

def back_low(kept, grad):
    return (low(grad),)
low.defvjp(low_keep, low_pass)
low_back.defvjp(back_keep, back_low)

def einsum_high(formula, left_side, right_side):
    return jnp.einsum(formula, left_side, right_side, precision=lax.Precision.HIGHEST)

def matmul_high(left_side, right_side):
    return jnp.dot(left_side, right_side, precision=lax.Precision.HIGHEST)

def householder_attention(queries, key_rows, values, raw_directions, beta_logits, length):
    seq_len, head_size = queries.shape
    block_size = SPAN
    blocks = seq_len // block_size
    position = jnp.arange(seq_len, dtype=jnp.int32)
    live_mask = (position < length).astype(jnp.float32)
    directions = raw_directions * lax.rsqrt(lax.optimization_barrier(jnp.sum(raw_directions * raw_directions, axis=-1, keepdims=True)) + 1e-06)
    strength = jax.nn.sigmoid(beta_logits) * live_mask
    query_blocks = queries.reshape(blocks, block_size, head_size)
    key_blocks = key_rows.reshape(blocks, block_size, head_size)
    direction_blocks = directions.reshape(blocks, block_size, head_size)
    strength_blocks = strength.reshape(blocks, block_size)
    inner_index = jnp.arange(block_size, dtype=jnp.int32)
    strict_below = (inner_index[:, None] > inner_index[None, :]).astype(jnp.float32)
    upto_mask = (inner_index[:, None] >= inner_index[None, :]).astype(jnp.float32)
    direction_gram = einsum_high('nsd,ntd->nst', direction_blocks, direction_blocks)
    negated = -(strength_blocks[:, :, None] * direction_gram * strict_below)
    inverse = jnp.eye(block_size, dtype=jnp.float32)[None, :, :] + negated
    power_term = negated
    for doubling in range(1, (block_size - 1).bit_length()):
        power_term = einsum_high('nst,ntu->nsu', power_term, power_term)
        inverse = inverse + einsum_high('nst,ntu->nsu', inverse, power_term)
    query_direction = einsum_high('nid,ntd->nit', query_blocks, direction_blocks) * upto_mask
    direction_key = einsum_high('nsd,njd->nsj', direction_blocks, key_blocks) * strict_below
    weighted = strength_blocks[:, :, None]
    update_rows = einsum_high('nts,nsd->ntd', inverse, weighted * direction_blocks)
    update_keys = einsum_high('nts,nsj->ntj', inverse, weighted * direction_key)
    moved_queries = query_blocks - einsum_high('nit,ntd->nid', query_direction, update_rows)
    moved_keys = key_blocks - einsum_high('ntj,ntd->njd', update_keys, direction_blocks)
    local_scores = einsum_high('nid,njd->nij', query_blocks, key_blocks) - einsum_high('nit,ntj->nij', query_direction, update_keys)
    scale = head_size ** (-0.5)

    def advance(carried, block_items):
        block_queries, block_keys, block_rows, block_directions, block_local, start_row = block_items
        across = einsum_high('id,jd->ij', block_queries, carried)
        across = lax.dynamic_update_slice_in_dim(across, block_local, start_row, 1)
        row_position = start_row + inner_index
        allowed = (position[None, :] <= row_position[:, None]) & (position[None, :] < length)
        scores = jnp.where(allowed, across * scale, -1e+30)
        row_max = lax.optimization_barrier(jnp.max(scores, axis=-1, keepdims=True))
        weights = jnp.exp(scores - row_max)
        weights = weights / lax.optimization_barrier(jnp.sum(weights, axis=-1, keepdims=True))
        block_out = einsum_high('ij,jd->id', weights, values)
        carried = carried - einsum_high('jt,td->jd', einsum_high('jd,td->jt', carried, block_rows), block_directions)
        carried = lax.dynamic_update_slice_in_dim(carried, block_keys, start_row, 0)
        return (carried, block_out)
    starts = jnp.arange(blocks, dtype=jnp.int32) * block_size
    initial = jnp.zeros((seq_len, head_size), jnp.float32)
    _, attended = lax.scan(jax.checkpoint(advance), initial, (moved_queries, moved_keys, update_rows, direction_blocks, local_scores, starts))
    return attended.reshape(seq_len, head_size)

def root_norm(features, scales):
    return features * lax.rsqrt(lax.optimization_barrier(jnp.mean(features * features, axis=-1, keepdims=True)) + 1e-06) * scales

def block_forward(inputs, query_proj, key_proj, value_proj, direction_proj, beta_proj, output_proj, gate_proj, up_proj, down_proj, gain_first, gain_second, slot_lengths):
    row_values = inputs.reshape(-1, D)
    slot_count = slot_lengths.shape[0]
    first_rows = low(root_norm(row_values, gain_first))
    queries = low_back(low(matmul_high(first_rows, query_proj)))
    key_rows = low_back(low(matmul_high(first_rows, key_proj)))
    values = low_back(low(matmul_high(first_rows, value_proj)))
    raw_directions = low_back(low(matmul_high(first_rows, direction_proj)))
    beta_logits = low_back(matmul_high(first_rows, beta_proj))

    def split_heads(tensor):
        return tensor.reshape(slot_count, LEN, HEADS, HEAD_DIM)

    def one_slot(slot_items):
        per_head = jax.vmap(householder_attention, in_axes=(1, 1, 1, 1, 1, None), out_axes=1)
        return per_head(slot_items[0], slot_items[1], slot_items[2], slot_items[3], slot_items[4], slot_items[5])
    kept_slot = jax.checkpoint(one_slot)

    def scan_step(carried, slot_items):
        return (carried, kept_slot(slot_items))
    slot_inputs = (split_heads(queries), split_heads(key_rows), split_heads(values), split_heads(raw_directions), beta_logits.reshape(slot_count, LEN, HEADS), slot_lengths)
    _, mixed = lax.scan(scan_step, jnp.zeros((), jnp.float32), slot_inputs)
    attended = low_back(low(mixed.reshape(-1, HEADS * HEAD_DIM)))
    middle = row_values + low_back(matmul_high(attended, output_proj))
    second_rows = low(root_norm(middle, gain_second))
    gate_values = low_back(matmul_high(second_rows, gate_proj))
    up_values = low_back(matmul_high(second_rows, up_proj))
    hidden = low(jax.nn.silu(gate_values) * up_values)
    result = middle + low_back(matmul_high(hidden, down_proj))
    return result.reshape(inputs.shape)

def reference(tokens, lengths, cotangent, q_weight, k_weight, v_weight, direction_weight, beta_weight, out_weight, gate_weight, up_weight, down_weight, norm_gain_one, norm_gain_two):
    slot_lengths = lengths.reshape(-1).astype(jnp.int32)
    floats = [array.astype(jnp.float32) for array in (tokens, q_weight, k_weight, v_weight, direction_weight, beta_weight, out_weight, gate_weight, up_weight, down_weight, norm_gain_one, norm_gain_two)]

    def forward(inputs, query_proj, key_proj, value_proj, direction_proj, beta_proj, output_proj, gate_proj, up_proj, down_proj, gain_first, gain_second):
        return block_forward(inputs, query_proj, key_proj, value_proj, direction_proj, beta_proj, output_proj, gate_proj, up_proj, down_proj, gain_first, gain_second, slot_lengths)
    result, pullback = jax.vjp(forward, floats[0], floats[1], floats[2], floats[3], floats[4], floats[5], floats[6], floats[7], floats[8], floats[9], floats[10], floats[11])
    gradients = pullback(cotangent.astype(jnp.float32))
    return (result.astype(jnp.bfloat16), gradients[0], gradients[1], gradients[2], gradients[3], gradients[4], gradients[5], gradients[6], gradients[7], gradients[8], gradients[9], gradients[10], gradients[11])
```

```python
import functools

import jax
import jax.numpy as jnp
from jax import lax
from jax.experimental import pallas as pl
from jax.experimental.pallas import tpu as pltpu
from jax.sharding import Mesh, PartitionSpec as P

HEAD_DIM = 128
TILE = 128
F32 = jnp.float32
BF16 = jnp.bfloat16
COST_SCALE = 2.5e+09
(
    ATTN_ROWS,
    OUT_ROWS,
    FFN_OWN,
    FFN_GIVE,
    COT,
    ATTN,
    FFN_TAKE,
    HOP,
    TOK,
    CHUNK,
    OUT,
    OUT_ALL,
    COT_OTHER,
    ATTEND,
    MIX,
    PROJECT,
    TURN_COT,
    MIDDLE,
    H2_OTHER,
    FEED,
    DH_OTHER,
    TURN_H2,
    GRAD_FAR,
    PLANE_SUM,
    SUM,
    FAR,
    GRAD_MIDDLE,
    MID,
    GRAD_NEAR,
    LAST,
    LAST_OTHER,
    NORM,
    SENT,
    OUT_GRAD,
    OUT_CORE,
    OUT_RS,
    OUTSUM,
    DOWN,
    DOWN_OTHER,
    BACK,
    DH,
    RING,
    ATTN_GRAD,
    ATTN_CORE,
    ATTN_RS,
    GAIN,
    INPUT,
    BLOCK_OUT,
    FINISH,
) = range(49)
PLAN = {
    "order": (
        (PROJECT, 0),
        (ATTEND, 0),
        TURN_COT,
        (PROJECT, 1),
        (ATTEND, 1),
        MIDDLE,
        (FEED, 0),
        TURN_H2,
        (FEED, 1),
        (GRAD_FAR, 1),
        (FEED, 2),
        (GRAD_FAR, 2),
        (FEED, 3),
        NORM,
        (GRAD_FAR, 3),
        OUT_GRAD,
        (BACK, 0),
        (DH, 0),
        DOWN,
        (GRAD_FAR, 0),
        (BACK, 1),
        (DH, 1),
        ATTN_GRAD,
        (GRAD_MIDDLE, 0),
        (INPUT, 0),
        BLOCK_OUT,
        LAST,
        (INPUT, 1),
        FINISH,
    ),
    "direct": (2,),
    "da_first": (0,),
    "whole": (1, 2, 3),
    "gates": {
        (TOK, 1, 3): ((ATTEND, 0),),
        (HOP, 1): ((TOK, 1, 3),),
        (HOP, 2): ((PROJECT, 1),),
        (HOP, 3): ((ATTEND, 1),),
        (CHUNK, 0, 0): (ATTN_ROWS,),
        OUT_ALL: ((PROJECT, 1),),
        (CHUNK, 3, 0): (MIDDLE,),
        (TOK, 0, 2): ((HOP, 0),),
        (CHUNK, 1, 0): ((ATTEND, 1),),
        OUT_RS: ((GRAD_FAR, 0),),
    },
    "pins": {
        (ATTEND, 1): ((CHUNK, 0, 0),),
        (GRAD_FAR, 0): ((RING, 0, 1),),
        (INPUT, 0): ((RING, 1, 2),),
        (DH, 0): ((SUM, 1),),
        (FEED, 1): ((MIX, 1, 1),),
        (DH, 1): ((RING, 0, 2),),
        ATTN_GRAD: ((RING, 0, 3),),
        (GRAD_MIDDLE, 0): ((RING, 1, 1), (SUM, 2)),
    },
}
QUERY, KEY, VALUE, RAW = [slice(i * HEAD_DIM, (i + 1) * HEAD_DIM) for i in range(4)]


def mm(left, right):
    return lax.dot_general(
        left.astype(BF16), right.astype(BF16), (((1,), (0,)), ((), ())), preferred_element_type=F32
    )


def mm_nt(left, right):
    return lax.dot_general(
        left.astype(BF16), right.astype(BF16), (((1,), (1,)), ((), ())), preferred_element_type=F32
    )


def mm_tn(left, right):
    return lax.dot_general(
        left.astype(BF16), right.astype(BF16), (((0,), (0,)), ((), ())), preferred_element_type=F32
    )


def tile_index():
    rows = lax.broadcasted_iota(jnp.int32, (TILE, TILE), 0)
    cols = lax.broadcasted_iota(jnp.int32, (TILE, TILE), 1)
    return rows, cols


def each(function, *lists):
    return [function(*items) for items in zip(*lists)]


def unit_directions(raw):
    raw = raw.astype(F32)
    inv_norm = lax.rsqrt(jnp.sum(raw * raw, axis=-1, keepdims=True) + 1e-06)
    return raw * inv_norm, inv_norm


def get_row(ref, row, cols):
    block = ref[:, cols]
    lines = lax.broadcasted_iota(jnp.int32, block.shape, 0)
    return jnp.sum(jnp.where(lines == row, block, 0.0), axis=0, keepdims=True)


def set_row(ref, row, cols, value):
    block = ref[:, cols]
    lines = lax.broadcasted_iota(jnp.int32, block.shape, 0)
    ref[:, cols] = jnp.where(lines == row, value, block)


def inverse_tiles(lower):
    rows, cols = tile_index()
    identity = (rows == cols).astype(F32)
    width = 8
    part = (rows // width == cols // width).astype(F32)
    power = each(lambda a: a * part, lower)
    result = each(lambda a: identity - a, power)
    reach = 2
    while reach < width:
        power = each(lambda a: mm(a, a), power)
        result = each(lambda a, b: a + mm(a, b), result, power)
        reach *= 2
    while width < TILE:
        corner = (
            (rows // (2 * width) == cols // (2 * width)) & (rows // width != cols // width)
        ).astype(F32)
        inner = each(lambda a, b: mm(a * corner, b), lower, result)
        result = each(lambda a, b: a - mm(a, b), result, inner)
        width *= 2
    return result


def forward_kernel(
    where_ref, length_ref, x_ref, logit_ref,
    out_ref, tt_ref, e_ref, g_ref, d_ref, mq_ref, state_ref, prob_ref,
    mk_ref, local_ref, run_ref,
):
    seq_len = x_ref.shape[0]
    tiles = seq_len // TILE
    length = length_ref[0]
    head = pl.program_id(0)
    rows, cols = tile_index()
    below = (rows > cols).astype(F32)
    upto = (rows >= cols).astype(F32)
    span = [pl.ds(n * TILE, TILE) for n in range(tiles)]
    group = min(tiles, 8)
    for first in range(0, tiles, group):
        part = list(range(first, first + group))
        units = [unit_directions(x_ref[span[n], RAW])[0].astype(BF16) for n in part]
        queries = [x_ref[span[n], QUERY] for n in part]
        keys = [x_ref[span[n], KEY] for n in part]
        position = lax.broadcasted_iota(jnp.int32, (1, TILE), 1)
        strength = [
            jnp.where(
                position + n * TILE < length,
                jax.nn.sigmoid(get_row(logit_ref, head, slice(n * TILE, (n + 1) * TILE))),
                0.0,
            )
            for n in part
        ]
        gram = each(lambda w: mm_nt(w, w) * below, units)
        inverse = inverse_tiles(each(lambda g, b: g * b, gram, strength))
        turned = each(lambda t: t.T, inverse)
        for n, t in zip(part, turned):
            tt_ref[span[n], :] = t.astype(BF16)
        upper = each(lambda t, b: (t * b).astype(BF16), turned, strength)
        cross = each(lambda w, k: (mm_nt(w, k) * below).astype(BF16), units, keys)
        seen = each(lambda q, w: (mm_nt(q, w) * upto).astype(BF16), queries, units)
        weight = each(lambda a, u: mm_nt(a, u).astype(BF16), seen, upper)
        slope = each(lambda u, w: mm(u, w).astype(BF16), upper, units)
        moved_q = each(lambda q, e, w: (q.astype(F32) - mm(e, w)).astype(BF16), queries, weight, units)
        local = each(lambda q, k, e, c: mm_nt(q, k) - mm(e, c), queries, keys, weight, cross)
        moved_k = each(lambda k, c, g: k.astype(F32) - mm_tn(c, g), keys, cross, slope)
        step = each(lambda w, g: mm_tn(w, g).astype(BF16), units, slope)
        for i, n in enumerate(part):
            e_ref[span[n], :] = weight[i]
            g_ref[span[n], :] = slope[i]
            d_ref[span[n], :] = step[i]
            mq_ref[span[n], :] = moved_q[i]
            local_ref[span[n], :] = local[i]
            mk_ref[span[n], :] = moved_k[i]
    scale = HEAD_DIM ** (-0.5)
    offset = 0
    for n in range(tiles):
        done = n * TILE
        if n:
            old = pl.ds(0, done)
            past = run_ref[old, :]
            past_low = past.astype(BF16)
            state_ref[pl.ds(offset, done), :] = past_low
            offset += done
            scores = jnp.concatenate(
                [mm_nt(mq_ref[span[n], :], past_low), local_ref[span[n], :]], axis=1
            )
            if n + 1 < tiles:
                run_ref[old, :] = past - mm(past_low, d_ref[span[n], :])
        else:
            scores = local_ref[span[n], :]
        if n + 1 < tiles:
            run_ref[span[n], :] = mk_ref[span[n], :]
        wide = done + TILE
        row_at = lax.broadcasted_iota(jnp.int32, (TILE, wide), 0) + done
        col_at = lax.broadcasted_iota(jnp.int32, (TILE, wide), 1)
        allowed = (col_at <= row_at) & (col_at < length)
        scores = jnp.where(allowed, scores * scale, -1e30)
        top = jnp.max(scores, axis=-1, keepdims=True)
        weights = jnp.exp(scores - top)
        weights = weights * (1.0 / jnp.sum(weights, axis=-1, keepdims=True))
        weights = weights.astype(BF16)
        prob_ref[0, span[n], pl.ds(0, wide)] = weights
        mixed = mm(weights, x_ref[pl.ds(0, wide), VALUE]).astype(out_ref.dtype)
        if len(out_ref.shape) == 2:
            out_ref[span[n], :] = mixed
        else:
            per = out_ref.shape[1] // TILE
            row = (n % per) * TILE
            out_ref[where_ref[12 + n // per], row : row + TILE, :] = mixed


def backward_kernel(
    grad_count, where_ref, length_ref, x_ref, logit_ref, *refs
):
    grad_refs, refs = refs[:grad_count], refs[grad_count:]
    (
    tt_ref, e_ref, g_ref, d_ref, mq_ref, state_ref, prob_ref,
    dx_ref, dlogit_ref,
    run_ref, value_ref, dmq_ref, dlocal_ref, dmk_ref, dstep_ref, do_ref,
    ) = refs
    part = grad_refs[0].shape[0]

    @pl.when(pl.program_id(0) == 0)
    def _():
        dlogit_ref[...] = jnp.zeros_like(dlogit_ref)

    for s, ref in enumerate(grad_refs):
        at = where_ref[8 + s] * part if grad_count > 1 else 0
        do_ref[pl.ds(pl.multiple_of(at, TILE), part), :] = ref[...]
    seq_len = x_ref.shape[0]
    tiles = seq_len // TILE
    length = length_ref[0]
    head = pl.program_id(0)
    rows, cols = tile_index()
    below = (rows > cols).astype(F32)
    upto = (rows >= cols).astype(F32)
    identity = (rows == cols).astype(F32)
    scale = HEAD_DIM ** (-0.5)
    span = [pl.ds(n * TILE, TILE) for n in range(tiles)]
    offset = TILE * (tiles * (tiles - 1) // 2)
    for n in reversed(range(tiles)):
        done = n * TILE
        wide = done + TILE
        old = pl.ds(0, done)
        grad_out = do_ref[span[n], :]
        weights = prob_ref[0, span[n], pl.ds(0, wide)]
        grad_w = mm_nt(grad_out, x_ref[pl.ds(0, wide), VALUE])
        weights_full = weights.astype(F32)
        mixed = weights_full * grad_w
        total = jnp.sum(mixed, axis=-1, keepdims=True)
        grad_s = ((mixed - weights_full * total) * scale).astype(BF16)
        back = mm_tn(weights, grad_out)
        if n + 1 < tiles:
            value_ref[pl.ds(0, wide), :] = value_ref[pl.ds(0, wide), :] + back
        else:
            value_ref[...] = back
        dlocal_ref[span[n], :] = grad_s[:, done:]
        if n + 1 < tiles:
            dmk_ref[span[n], :] = run_ref[span[n], :].astype(BF16)
        else:
            dmk_ref[span[n], :] = jnp.zeros((TILE, HEAD_DIM), BF16)
        if n:
            offset -= done
            past = state_ref[pl.ds(offset, done), :]
            grad_far = grad_s[:, :done]
            dmq_ref[span[n], :] = mm(grad_far, past).astype(BF16)
            fresh = mm_tn(grad_far, mq_ref[span[n], :])
            if n + 1 < tiles:
                carried = run_ref[old, :]
                carried_low = carried.astype(BF16)
                dstep_ref[span[n], :] = (-mm_tn(past, carried_low)).astype(BF16)
                run_ref[old, :] = carried - mm_nt(carried_low, d_ref[span[n], :]) + fresh
            else:
                dstep_ref[span[n], :] = jnp.zeros((TILE, HEAD_DIM), BF16)
                run_ref[old, :] = fresh
        else:
            dmq_ref[span[n], :] = jnp.zeros((TILE, HEAD_DIM), BF16)
            dstep_ref[span[n], :] = jnp.zeros((TILE, HEAD_DIM), BF16)
    dx_ref[:, VALUE] = value_ref[...].astype(dx_ref.dtype)
    group = min(tiles, 8)
    for first in range(0, tiles, group):
        part = list(range(first, first + group))
        pairs = [unit_directions(x_ref[span[n], RAW]) for n in part]
        units = [p[0].astype(BF16) for p in pairs]
        queries = [x_ref[span[n], QUERY] for n in part]
        keys = [x_ref[span[n], KEY] for n in part]
        position = lax.broadcasted_iota(jnp.int32, (1, TILE), 1)
        gates = [
            jax.nn.sigmoid(get_row(logit_ref, head, slice(n * TILE, (n + 1) * TILE))) for n in part
        ]
        live = [(position + n * TILE < length).astype(F32) for n in part]
        strength = each(lambda s, m: s * m, gates, live)
        turned = [tt_ref[span[n], :] for n in part]
        weight = [e_ref[span[n], :] for n in part]
        slope = [g_ref[span[n], :] for n in part]
        dlocal = [dlocal_ref[span[n], :] for n in part]
        dmq = [dmq_ref[span[n], :] for n in part]
        dmk = [dmk_ref[span[n], :] for n in part]
        dstep = [dstep_ref[span[n], :] for n in part]
        gram = each(lambda w: mm_nt(w, w) * below, units)
        cross = each(lambda w, k: (mm_nt(w, k) * below).astype(BF16), units, keys)
        seen = each(lambda q, w: (mm_nt(q, w) * upto).astype(BF16), queries, units)
        upper = each(lambda t, b: (t.astype(F32) * b).astype(BF16), turned, strength)
        dweight = each(
            lambda dm, w, dl, c: (-(mm_nt(dm, w) + mm_nt(dl, c))).astype(BF16),
            dmq, units, dlocal, cross,
        )
        dcross = each(
            lambda e, dl, g, dm: ((-(mm_tn(e, dl) + mm_nt(g, dm))) * below).astype(BF16),
            weight, dlocal, slope, dmk,
        )
        dslope = each(
            lambda w, ds, c, dm: (mm(w, ds) - mm(c, dm)).astype(BF16), units, dstep, cross, dmk
        )
        dinv = each(
            lambda a, de, w, dg: (mm_tn(a, de) + mm_nt(w, dg)).astype(BF16),
            seen, dweight, units, dslope,
        )
        dseen = each(lambda de, u: (mm(de, u) * upto).astype(BF16), dweight, upper)
        inner = each(lambda d, t: mm(d, t), dinv, turned)
        dlower = each(lambda u, h: -mm(u, h) * below, upper, inner)
        dgram = each(lambda d, b: (d * b).astype(BF16), dlower, strength)
        dunit = each(
            lambda e, dm, g, ds, u, dg: mm_nt(g, ds) - mm_tn(e, dm) + mm_tn(u, dg),
            weight, dmq, slope, dstep, upper, dslope,
        )
        dunit = each(
            lambda acc, da, q, dc, k, dg, w: acc
            + mm_tn(da, q) + mm(dc, k) + mm(dg, w) + mm_tn(dg, w),
            dunit, dseen, queries, dcross, keys, dgram, units,
        )
        for i, n in enumerate(part):
            dx_ref[span[n], QUERY] = (
                dmq[i].astype(F32) + mm(dlocal[i], keys[i]) + mm(dseen[i], units[i])
            ).astype(dx_ref.dtype)
            dx_ref[span[n], KEY] = (
                dmk[i].astype(F32) + mm_tn(dlocal[i], queries[i]) + mm_tn(dcross[i], units[i])
            ).astype(dx_ref.dtype)
            raw = x_ref[span[n], RAW].astype(F32)
            inv_norm = pairs[i][1]
            along = jnp.sum(raw * dunit[i], axis=-1, keepdims=True)
            dx_ref[span[n], RAW] = (
                inv_norm * dunit[i] - raw * (inv_norm * inv_norm * inv_norm) * along
            ).astype(dx_ref.dtype)
            dstrength = jnp.sum(
                identity * inner[i] + dlower[i] * gram[i], axis=0, keepdims=True
            )
            set_row(
                dlogit_ref,
                head,
                slice(n * TILE, (n + 1) * TILE),
                dstrength * gates[i] * (1.0 - gates[i]) * live[i],
            )


def saved_shapes(heads, seq_len):
    tiles = seq_len // TILE
    flat = jax.ShapeDtypeStruct((seq_len, heads * HEAD_DIM), BF16)
    state = jax.ShapeDtypeStruct((TILE * max(1, tiles * (tiles - 1) // 2), heads * HEAD_DIM), BF16)
    prob = jax.ShapeDtypeStruct((heads, seq_len, seq_len), BF16)
    return [flat] * 5 + [state, prob]


def saved_specs(heads, seq_len):
    tiles = seq_len // TILE
    flat = pl.BlockSpec((seq_len, HEAD_DIM), lambda h: (0, h))
    state = pl.BlockSpec((TILE * max(1, tiles * (tiles - 1) // 2), HEAD_DIM), lambda h: (0, h))
    prob = pl.BlockSpec((1, seq_len, seq_len), lambda h: (h, 0, 0))
    return [flat] * 5 + [state, prob]


def packed_spec(seq_len):
    return pl.BlockSpec((seq_len, 4 * HEAD_DIM), lambda h: (0, h))


def attention_forward(where, length, projected, logits):
    seq_len = projected.shape[0]
    heads = projected.shape[1] // (4 * HEAD_DIM)
    flat = pl.BlockSpec((seq_len, HEAD_DIM), lambda h: (0, h))
    return pl.pallas_call(
        forward_kernel,
        grid=(heads,),
        in_specs=[pl.BlockSpec(memory_space=pltpu.SMEM)] * 2
        + [packed_spec(seq_len)]
        + [pl.BlockSpec(logits.shape, lambda h: (0, 0))],
        out_specs=[
            flat
            if where is None
            else pl.BlockSpec((4, seq_len // 4, HEAD_DIM), lambda h: (0, 0, h))
        ]
        + saved_specs(heads, seq_len),
        out_shape=[
            jax.ShapeDtypeStruct(
                (seq_len, heads * HEAD_DIM)
                if where is None
                else (4, seq_len // 4, heads * HEAD_DIM),
                BF16,
            )
        ]
        + saved_shapes(heads, seq_len),
        scratch_shapes=[
            pltpu.VMEM((seq_len, HEAD_DIM), F32),
            pltpu.VMEM((seq_len, TILE), F32),
            pltpu.VMEM((seq_len, HEAD_DIM), F32),
        ],
        name="attention_forward",
        compiler_params=pltpu.CompilerParams(vmem_limit_bytes=56 * 1024 * 1024),
        cost_estimate=cost(21),
    )(length if where is None else where, length, projected, logits)


def attention_backward(where, length, projected, logits, grad_out, batch, saved):
    seq_len = projected.shape[0]
    heads = projected.shape[1] // (4 * HEAD_DIM)
    flat = pl.BlockSpec((seq_len, HEAD_DIM), lambda h: (0, h))
    row = pl.BlockSpec(logits.shape, lambda h: (0, 0))
    result = pl.pallas_call(
        functools.partial(backward_kernel, len(grad_out)),
        grid=(heads,),
        in_specs=[pl.BlockSpec(memory_space=pltpu.SMEM)] * 2
        + [packed_spec(seq_len), row]
        + [pl.BlockSpec((None, seq_len // len(grad_out), HEAD_DIM), lambda h: (batch, 0, h))]
        * len(grad_out)
        + saved_specs(heads, seq_len),
        out_specs=[packed_spec(seq_len), row],
        out_shape=[
            jax.ShapeDtypeStruct(projected.shape, BF16),
            jax.ShapeDtypeStruct(logits.shape, F32),
        ],
        scratch_shapes=[
            pltpu.VMEM((seq_len, HEAD_DIM), F32),
            pltpu.VMEM((seq_len, HEAD_DIM), F32),
            pltpu.VMEM((seq_len, HEAD_DIM), BF16),
            pltpu.VMEM((seq_len, TILE), BF16),
            pltpu.VMEM((seq_len, HEAD_DIM), BF16),
            pltpu.VMEM((seq_len, HEAD_DIM), BF16),
            pltpu.VMEM((seq_len, HEAD_DIM), BF16),
        ],
        name="attention_backward",
        compiler_params=pltpu.CompilerParams(vmem_limit_bytes=56 * 1024 * 1024),
        cost_estimate=cost(22),
    )(
        length if where is None else where,
        length,
        projected,
        logits,
        *grad_out,
        *saved,
    )
    return result[0], result[1]


def cost(microseconds):
    return pl.CostEstimate(
        flops=int(microseconds * COST_SCALE), bytes_accessed=1, transcendentals=0
    )


def params(mebibytes=56):
    return pltpu.CompilerParams(vmem_limit_bytes=mebibytes * 1024 * 1024)


def column(index, width):
    return pl.ds(pl.multiple_of(index * width, 128), width)


def row_norm(rows):
    return lax.rsqrt(jnp.mean(rows * rows, axis=-1, keepdims=True) + 1e-06)


def project_kernel(where_ref, p0, p1, p2, p3, w_ref, small_ref, gain_ref, h_ref, out_ref, logit_ref):
    def work(piece):
        rows = piece[...].astype(F32)
        normed = (rows * row_norm(rows) * gain_ref[...]).astype(BF16)
        h_ref[...] = normed
        for at in range(0, out_ref.shape[1], 512):
            out_ref[:, at : at + 512] = mm(normed, w_ref[:, at : at + 512]).astype(BF16)
        logit_ref[...] = mm_nt(small_ref[...], normed)

    for s, piece in enumerate((p0, p1, p2, p3)):
        pl.when(pl.program_id(0) == s)(functools.partial(work, piece))


def project(where, pieces, weight, small, gain, columns):
    part, width = pieces[0].shape
    rows = part * len(pieces)
    whole = lambda shape: pl.BlockSpec(shape, lambda i, w: (0, 0))
    return pl.pallas_call(
        project_kernel,
        grid_spec=pltpu.PrefetchScalarGridSpec(
            num_scalar_prefetch=1,
            grid=(len(pieces),),
            in_specs=[whole((part, width))] * 4
            + [whole(weight.shape), whole(small.shape), whole((1, width))],
            out_specs=[
                pl.BlockSpec((part, width), lambda i, w: (w[4 + i], 0)),
                pl.BlockSpec((part, columns), lambda i, w: (w[4 + i], 0)),
                pl.BlockSpec((small.shape[0], part), lambda i, w: (0, w[4 + i])),
            ],
        ),
        out_shape=[
            jax.ShapeDtypeStruct((rows, width), BF16),
            jax.ShapeDtypeStruct((rows, columns), BF16),
            jax.ShapeDtypeStruct((small.shape[0], rows), F32),
        ],
        name="project_rows",
        compiler_params=params(),
        cost_estimate=cost(9),
    )(where, *pieces, weight, small, gain)


def turn_kernel(where_ref, own_ref, other_ref, a_ref, b_ref, t_ref):
    own, other = own_ref[...], other_ref[...]
    a_ref[...] = own
    b_ref[...] = other
    rows = own.shape[0]
    t_ref[:, :rows] = own.T
    t_ref[:, rows:] = other.T


def turn_only_kernel(where_ref, own_ref, other_ref, t_ref):
    rows = own_ref.shape[0]
    t_ref[:, :rows] = own_ref[...].T
    t_ref[:, rows:] = other_ref[...].T


def turned(where, own, other, reorder):
    rows, width = own.shape
    block = width // 4
    place_in = (lambda i, w: (0, w[i])) if reorder else (lambda i, w: (0, i))
    flat = pl.BlockSpec((rows, block), lambda i, w: (0, i))
    tall = pl.BlockSpec((block, 2 * rows), lambda i, w: (i, 0))
    tall_shape = jax.ShapeDtypeStruct((width, 2 * rows), BF16)
    same = jax.ShapeDtypeStruct((rows, width), BF16)
    return pl.pallas_call(
        turn_kernel if reorder else turn_only_kernel,
        grid_spec=pltpu.PrefetchScalarGridSpec(
            num_scalar_prefetch=1,
            grid=(4,),
            in_specs=[pl.BlockSpec((rows, block), place_in)] * 2,
            out_specs=[flat, flat, tall] if reorder else [tall],
        ),
        out_shape=[same, same, tall_shape] if reorder else [tall_shape],
        name="turn_rows",
        compiler_params=params(),
        cost_estimate=cost(3),
    )(where, own, other)


def gather_pieces(refs, scratch, count):
    part, inner = refs[0].shape
    for i, ref in enumerate(refs):
        batch, s = i // count, i % count
        scratch[batch * part : (batch + 1) * part, s * inner : (s + 1) * inner] = ref[...]


def assemble(where_ref, block_ref, scratch):
    rows, inner = block_ref.shape[2:]
    for c in range(2):
        for s in range(4):
            scratch[c * rows : (c + 1) * rows, s * inner : (s + 1) * inner] = block_ref[c, s]


def middle_kernel(pieces, where_ref, *refs):
    att_refs = refs[:pieces]
    w_ref, x_ref, gain_ref, mid_ref, h_ref, att, total, gains, weight = refs[pieces:]
    step = pl.program_id(0)

    @pl.when(step == 0)
    def _():
        gather_pieces(att_refs, att, 4)
        total[...] = jnp.zeros_like(total)

    assemble(where_ref, w_ref, weight)
    block = weight.shape[0]
    mid = x_ref[...].astype(F32) + mm_nt(att[...], weight[...])
    at = column(step, block)
    mid_ref[:, at] = mid
    gains[:, at] = jnp.broadcast_to(gain_ref[...], (8, block))
    total[...] += jnp.broadcast_to(jnp.sum(mid * mid, axis=-1, keepdims=True), total.shape)

    @pl.when(step == 3)
    def _():
        scale = lax.rsqrt(total[:, :1] * (1.0 / (4 * block)) + 1e-06)
        h_ref[...] = (mid_ref[...] * scale * gains[:1, :]).astype(BF16)


def middle_rows(where, pieces, out_all, rows_low, gain):
    rows, width = rows_low.shape
    block = width // 4
    part, inner = pieces[0].shape
    full = pl.BlockSpec((rows, width), lambda i, w: (0, 0))
    return pl.pallas_call(
        functools.partial(middle_kernel, len(pieces)),
        grid_spec=pltpu.PrefetchScalarGridSpec(
            num_scalar_prefetch=1,
            grid=(4,),
            in_specs=[pl.BlockSpec((part, inner), lambda i, w: (0, 0))] * len(pieces)
            + [
                pl.BlockSpec((2,) + out_all.shape[1:], lambda i, w: (w[i], 0, 0, 0)),
                pl.BlockSpec((rows, block), lambda i, w: (0, w[i])),
                pl.BlockSpec((1, block), lambda i, w: (0, w[i])),
            ],
            out_specs=[full, full],
            scratch_shapes=[
                pltpu.VMEM((rows, 4 * inner), BF16),
                pltpu.VMEM((rows, 128), F32),
                pltpu.VMEM((8, width), F32),
                pltpu.VMEM((block, 4 * inner), BF16),
            ],
        ),
        out_shape=[
            jax.ShapeDtypeStruct((rows, width), F32),
            jax.ShapeDtypeStruct((rows, width), BF16),
        ],
        name="middle_rows",
        compiler_params=params(),
        cost_estimate=cost(5),
    )(where, *pieces, out_all, rows_low, gain)


def load_pieces(where_ref, pieces, weight, sems, base, cols):
    copies = []
    at = 0
    for i in range(len(pieces) if len(pieces) > 1 else 4):
        if len(pieces) > 1:
            piece = pieces[i]
            height = piece.shape[0]
            rows = pl.ds(0, height)
        else:
            piece = pieces[0]
            height = piece.shape[0] // 4
            rows = pl.ds(pl.multiple_of(where_ref[i] * height, 128), height)
        copies.append(
            pltpu.make_async_copy(
                piece.at[rows, cols], weight.at[pl.ds(at, height), :], sems.at[base + i]
            )
        )
        at += height
    return copies


def store(ref, cols, value):
    ref[:, cols] = value.astype(ref.dtype)


def feed_kernel(units, first, last, where_ref, *refs):
    h_own, h_other, c_own, c_other = refs[:4]
    pieces = refs[4 : len(refs) - (4 + (0 if first else 1) + (1 if last else 0))]
    rest = refs[4 + len(pieces) :]
    if not first:
        dh_sum, rest = rest[0], rest[1:]
    act_ref, *dh_refs, weight, sems = rest
    step = pl.program_id(0)

    @pl.when(step == 0)
    def _():
        copies = load_pieces(
            where_ref, pieces, weight, sems, 0, pl.ds(0, weight.shape[1])
        )
        for copy in copies:
            copy.start()
        for copy in copies:
            copy.wait()

    mine = step < 2
    pair = 2 * units
    h = jnp.where(mine, h_own[...], h_other[...])
    c = jnp.where(mine, c_own[...], c_other[...])
    for at in range(0, units, 256):
        cols = slice(at, at + 256)
        gate = mm(h, weight[:, cols])
        up = mm(h, weight[:, units + at : units + at + 256])
        dhidden = mm(c, weight[:, pair + at : pair + at + 256])
        sig = jax.nn.sigmoid(gate)
        silu = gate * sig
        act_ref[:, pair + at : pair + at + 256] = (silu * up).astype(BF16)
        act_ref[:, cols] = (dhidden * up * (sig + silu * (1.0 - sig))).astype(BF16)
        act_ref[:, units + at : units + at + 256] = (dhidden * silu).astype(BF16)
    width = weight.shape[0]
    act = act_ref[:, :pair]
    for at in range(0, width, 512):
        cols = slice(at, at + 512)
        dh = mm_nt(act, weight[cols, :pair])
        if not first:
            dh = dh + dh_sum[:, cols]
        if last:
            pl.when(mine)(functools.partial(store, dh_refs[0], cols, dh))
            pl.when(jnp.logical_not(mine))(functools.partial(store, dh_refs[1], cols, dh))
        else:
            dh_refs[0][:, cols] = dh


def feed_forward_part(where, h2, cot, pieces, total, last):
    rows, width = h2[0].shape
    columns = pieces[0].shape[1]
    tile = rows // 2
    first = total is None
    own = pl.BlockSpec((tile, width), lambda i: (jnp.minimum(i, 1), 0))
    other = pl.BlockSpec((tile, width), lambda i: (jnp.maximum(i - 2, 0), 0))
    flat = pl.BlockSpec((tile, width), lambda i: (i, 0))
    whole = pl.BlockSpec(memory_space=pl.ANY)
    sums = (
        [jax.ShapeDtypeStruct((rows, width), F32), jax.ShapeDtypeStruct((rows, width), BF16)]
        if last
        else [jax.ShapeDtypeStruct((2 * rows, width), F32)]
    )
    return pl.pallas_call(
        functools.partial(feed_kernel, columns // 3, first, last),
        grid=(4,),
        in_specs=[pl.BlockSpec(memory_space=pltpu.SMEM), own, other, own, other]
        + [whole] * len(pieces)
        + ([] if first else [flat]),
        out_specs=[pl.BlockSpec((tile, columns), lambda i: (i, 0))]
        + ([own, other] if last else [flat]),
        out_shape=[jax.ShapeDtypeStruct((2 * rows, columns), BF16)] + sums,
        scratch_shapes=[
            pltpu.VMEM((width, columns), BF16),
            pltpu.SemaphoreType.DMA((max(4, len(pieces)),)),
        ],
        input_output_aliases={} if first or last else {5 + len(pieces): 1},
        name="feed_forward",
        compiler_params=params(),
        cost_estimate=cost(15),
    )(where, *h2, *cot, *pieces, *([] if first else [total]))


def down_kernel(counts, where_ref, *refs):
    chunks = len(counts)
    acts = refs[:chunks]
    pieces = refs[chunks : chunks + sum(counts)]
    own_ref, other_ref, weight, sems = refs[chunks + sum(counts) :]
    units = weight.shape[2]
    step = pl.program_id(0)

    @pl.when(step == 0)
    def _():
        copies = []
        i = 0
        for c, count in enumerate(counts):
            copies += load_pieces(
                where_ref,
                pieces[i : i + count],
                weight.at[c],
                sems,
                len(copies),
                pl.ds(2 * units, units),
            )
            i += count
        for copy in copies:
            copy.start()
        for copy in copies:
            copy.wait()

    for at in range(0, weight.shape[1], 512):
        cols = slice(at, at + 512)
        total = mm_nt(acts[0][...], weight[0, cols, :])
        for c in range(1, chunks):
            total = total + mm_nt(acts[c][...], weight[c, cols, :])
        pl.when(step == 0)(functools.partial(store, own_ref, cols, total))
        pl.when(step == 1)(functools.partial(store, other_ref, cols, total))


def down_rows(where, acts, chunks, width):
    rows = acts[0].shape[0] // 2
    tile = rows
    units = acts[0].shape[1] // 3
    counts = tuple(len(pieces) for pieces in chunks)
    own = pl.BlockSpec((tile, width), lambda i: (0, 0))
    other = own
    return pl.pallas_call(
        functools.partial(down_kernel, counts),
        grid=(2,),
        in_specs=[pl.BlockSpec(memory_space=pltpu.SMEM)]
        + [pl.BlockSpec((tile, units), lambda i: (i, 2))] * len(acts)
        + [pl.BlockSpec(memory_space=pl.ANY)] * sum(counts),
        out_specs=[own, other],
        out_shape=[
            jax.ShapeDtypeStruct((rows, width), F32),
            jax.ShapeDtypeStruct((rows, width), BF16),
        ],
        scratch_shapes=[
            pltpu.VMEM((len(acts), width, units), BF16),
            pltpu.SemaphoreType.DMA((sum(max(4, count) for count in counts),)),
        ],
        name="down_rows",
        compiler_params=params(),
        cost_estimate=cost(10),
    )(where, *acts, *[piece for pieces in chunks for piece in pieces])


def whole_grad_kernel(where_ref, h_ref, c_ref, act, out_ref):
    def work(left):
        value = mm(left[...], act[...]).astype(out_ref.dtype)
        height = value.shape[0] // 2
        for b in range(2):
            at = pl.multiple_of(((where_ref[0] & 1) ^ b) * height, 128)
            out_ref[pl.ds(at, height), :] = value[b * height : (b + 1) * height]

    pl.when(pl.program_id(0) < 2)(functools.partial(work, h_ref))
    pl.when(pl.program_id(0) == 2)(functools.partial(work, c_ref))


def whole_weight_grads(where, h2_t, cot_t, act):
    width, rows = h2_t.shape
    columns = act.shape[1]
    third = columns // 3
    height = width // 2
    return pl.pallas_call(
        whole_grad_kernel,
        grid_spec=pltpu.PrefetchScalarGridSpec(
            num_scalar_prefetch=1,
            grid=(3, 2),
            in_specs=[
                pl.BlockSpec((height, rows), lambda i, j, w: (jnp.where(i < 2, j, 1), 0)),
                pl.BlockSpec((height, rows), lambda i, j, w: (jnp.where(i < 2, 0, j), 0)),
                pl.BlockSpec((rows, third), lambda i, j, w: (0, i)),
            ],
            out_specs=pl.BlockSpec((height, third), lambda i, j, w: ((w[0] >> 1) ^ j, i)),
        ),
        out_shape=jax.ShapeDtypeStruct((width, columns), BF16),
        name="whole_grads",
        compiler_params=params(),
        cost_estimate=cost(10),
    )(where, h2_t, cot_t, act)


def last_grad_kernel(pair, where_ref, h_ref, c_ref, act, *refs):
    added, (own_ref, other_ref, total) = refs[:-3], refs[-3:]
    for cols, left in ((slice(0, pair), h_ref), (slice(pair, None), c_ref)):
        value = mm(left[...], act[:, cols])
        for term in added:
            value = value + term[:, cols].astype(F32)
        total[:, cols] = value
    rows = own_ref.shape[0]
    own_ref[...] = total[pl.ds(pl.multiple_of(where_ref[16] * rows, 64), rows), :]
    other = pl.ds(pl.multiple_of((1 - where_ref[16]) * rows, 64), rows)
    other_ref[...] = total[other, :].astype(BF16)


def last_weight_grads(where, h2_t, cot_t, act, added):
    width, rows = h2_t.shape
    columns = act.shape[1]
    height = width // 4
    left = pl.BlockSpec((height, rows), lambda i: (0, 0))
    tile = pl.BlockSpec((height, columns), lambda i: (0, 0))
    half = pl.BlockSpec((height // 2, columns), lambda i: (0, 0))
    return pl.pallas_call(
        functools.partial(last_grad_kernel, 2 * columns // 3),
        grid=(1,),
        in_specs=[pl.BlockSpec(memory_space=pltpu.SMEM), left, left]
        + [pl.BlockSpec((rows, columns), lambda i: (0, 0))]
        + [tile] * len(added),
        out_specs=[half, half],
        out_shape=[
            jax.ShapeDtypeStruct((height // 2, columns), F32),
            jax.ShapeDtypeStruct((height // 2, columns), BF16),
        ],
        scratch_shapes=[pltpu.VMEM((height, columns), F32)],
        name="last_weight_grad",
        compiler_params=params(),
        cost_estimate=cost(4),
    )(where, h2_t, cot_t, act, *[term for term, _ in added])


def finish_kernel(where_ref, own_ref, recv_ref, *outs):
    half = own_ref.shape[1] // 3
    for i, out in enumerate(outs):
        cols = slice(i * half, (i + 1) * half)
        out[:, column(where_ref[16], half)] = own_ref[:, cols]
        out[:, column(1 - where_ref[16], half)] = recv_ref[:, cols].astype(F32)


def finish_grads(where, own, recv):
    rows, columns = own.shape
    flat = pl.BlockSpec((rows, columns), lambda i: (0, 0))
    wide = pl.BlockSpec((rows, 2 * columns // 3), lambda i: (0, 0))
    return pl.pallas_call(
        finish_kernel,
        grid=(1,),
        in_specs=[pl.BlockSpec(memory_space=pltpu.SMEM), flat, flat],
        out_specs=[wide] * 3,
        out_shape=[jax.ShapeDtypeStruct((rows, 2 * columns // 3), F32)] * 3,
        name="finish_grads",
        compiler_params=params(),
        cost_estimate=cost(2),
    )(where, own, recv)


def grad_kernel(plan, *refs):
    count = len(plan)
    hs, cs, act = refs[:count], refs[count : 2 * count], refs[2 * count]
    extra = list(refs[2 * count + 1 : -1])
    out_ref = refs[-1]
    height = hs[0].shape[0]

    def work(lefts):
        at = 0
        for i, terms in enumerate(plan):
            value = mm(lefts[i][...], act[...])
            for term in extra[at : at + terms]:
                value = value + term[...].astype(F32)
            at += terms
            out_ref[i * height : (i + 1) * height, :] = value.astype(out_ref.dtype)

    pl.when(pl.program_id(0) < 2)(functools.partial(work, hs))
    pl.when(pl.program_id(0) == 2)(functools.partial(work, cs))


def weight_grads(h2_t, cot_t, act, blocks, added):
    width, rows = h2_t.shape
    columns = act.shape[1]
    height = width // 4
    third = columns // 3
    whole = len(blocks) * height
    if blocks == [2, 3]:
        height, blocks, added = 2 * height, [1], [[]]
    left = [pl.BlockSpec((height, rows), lambda i, at=at: (at, 0)) for at in blocks]
    terms = [term for group in added for term in group]
    tiles = [pl.BlockSpec((height, third), lambda i, at=at: (at, i)) for _, at in terms]
    return pl.pallas_call(
        functools.partial(grad_kernel, tuple(len(g) for g in added)),
        grid=(3,),
        in_specs=left + left + [pl.BlockSpec((rows, third), lambda i: (0, i))] + tiles,
        out_specs=pl.BlockSpec((whole, third), lambda i: (0, i)),
        out_shape=jax.ShapeDtypeStruct((whole, columns), BF16),
        name="weight_grads",
        compiler_params=params(),
        cost_estimate=cost(1 + whole // 192),
    )(*([h2_t] * len(blocks)), *([cot_t] * len(blocks)), act, *[term for term, _ in terms])


def norm_two_kernel(
    where_ref, own_ref, recv_ref, mid_ref, cot_ref, gain_ref, w_ref,
    dmid_ref, dm_ref, datt_ref, dgain_ref, weight,
):
    block = gain_ref.shape[1] // 4
    mid = mid_ref[...]
    scale = row_norm(mid)
    gain = jnp.concatenate([gain_ref[:, column(where_ref[j], block)] for j in range(4)], axis=1)
    upstream = own_ref[...] + recv_ref[...].astype(F32)
    weighted = upstream * gain
    inner = jnp.mean(mid * weighted, axis=-1, keepdims=True)
    grad = cot_ref[...].astype(F32) + scale * weighted - mid * (scale * scale * scale) * inner
    dmid_ref[...] = grad
    low = grad.astype(BF16)
    dm_ref[...] = low
    dgain = jnp.sum(upstream * mid * scale, axis=0, keepdims=True)

    @pl.when(pl.program_id(0) == 0)
    def _():
        dgain_ref[...] = jnp.zeros_like(dgain_ref)

    for j in range(4):
        at = column(where_ref[j], block)
        dgain_ref[0:1, at] = dgain_ref[0:1, at] + dgain[:, j * block : (j + 1) * block]
    total = None
    for j in range(4):
        for c in range(2):
            for s in range(4):
                rows, inner_width = w_ref.shape[2:]
                weight[c * rows : (c + 1) * rows, s * inner_width : (s + 1) * inner_width] = w_ref[
                    2 * where_ref[j] + c, s
                ]
        term = mm(low[:, j * block : (j + 1) * block], weight[...])
        total = term if total is None else total + term
    inner_width = datt_ref.shape[3]
    for s in range(4):
        datt_ref[s, 0] = total[:, s * inner_width : (s + 1) * inner_width].astype(BF16)


def norm_two(where, own, recv, middle, cot, gain, out_all, count):
    rows, width = middle.shape
    part = rows // count
    inner = out_all.shape[3]
    flat = pl.BlockSpec((part, width), lambda i, w: (i, 0))
    row = pl.BlockSpec((1, width), lambda i, w: (0, 0))
    return pl.pallas_call(
        norm_two_kernel,
        grid_spec=pltpu.PrefetchScalarGridSpec(
            num_scalar_prefetch=1,
            grid=(count,),
            in_specs=[flat] * 4
            + [row, pl.BlockSpec(out_all.shape, lambda i, w: (0, 0, 0, 0))],
            out_specs=[
                flat,
                flat,
                pl.BlockSpec((4, 1, part, inner), lambda i, w: (0, i, 0, 0)),
                row,
            ],
            scratch_shapes=[pltpu.VMEM((width // 4, 4 * inner), BF16)],
        ),
        out_shape=[
            jax.ShapeDtypeStruct((rows, width), F32),
            jax.ShapeDtypeStruct((rows, width), BF16),
            jax.ShapeDtypeStruct((4, count, part, inner), BF16),
            jax.ShapeDtypeStruct((1, width), F32),
        ],
        name="norm_two",
        compiler_params=params(),
        cost_estimate=cost(6),
    )(where, own, recv, middle, cot, gain, out_all)


def dh1_kernel(where_ref, d_ref, l_ref, h_ref, w_ref, small_ref, gain_ref, out_ref, dgain_ref):
    columns = d_ref.shape[1]
    step = pl.program_id(0)

    @pl.when(step == 0)
    def _():
        dgain_ref[...] = jnp.zeros_like(dgain_ref)

    grads = d_ref[...]
    for at in range(0, w_ref.shape[0], 512):
        cols = slice(at, at + 512)
        total = mm_nt(grads, w_ref[cols, :columns]) + mm_tn(l_ref[...], small_ref[:, cols])
        out_ref[0, :, cols] = total.astype(BF16)
        part = jnp.sum(total * h_ref[:, cols].astype(F32), axis=0, keepdims=True)
        dgain_ref[:, cols] = dgain_ref[:, cols] + part

    @pl.when(step == 3)
    def _():
        dgain_ref[...] = dgain_ref[...] / gain_ref[...]


def dh1_pieces(where, dprojected, dlogits, normed, weight, small, gain):
    rows, columns = dprojected.shape
    width = weight.shape[0]
    part = rows // 4
    whole = lambda shape: pl.BlockSpec(shape, lambda i, w: (0, 0))
    return pl.pallas_call(
        dh1_kernel,
        grid_spec=pltpu.PrefetchScalarGridSpec(
            num_scalar_prefetch=1,
            grid=(4,),
            in_specs=[
                pl.BlockSpec((part, columns), lambda i, w: (w[7 - i], 0)),
                pl.BlockSpec((dlogits.shape[0], part), lambda i, w: (0, w[7 - i])),
                pl.BlockSpec((part, width), lambda i, w: (w[7 - i], 0)),
                whole(weight.shape),
                whole(small.shape),
                whole(gain.shape),
            ],
            out_specs=[
                pl.BlockSpec((1, part, width), lambda i, w: (3 - i, 0, 0)),
                whole(gain.shape),
            ],
        ),
        out_shape=[
            jax.ShapeDtypeStruct((4, part, width), BF16),
            jax.ShapeDtypeStruct(gain.shape, F32),
        ],
        name="dh1_rows",
        compiler_params=params(),
        cost_estimate=cost(0.008),
    )(where, dprojected, dlogits, normed, weight, small, gain)


def store_cores(where_ref, out_ref, cols, values):
    rows = values.shape[0] // 2
    for c in range(2):
        out_ref[jnp.where(where_ref[16] == c, 0, 1), :, cols] = values[
            c * rows : (c + 1) * rows
        ]


def attn_grad_kernel(count, beta, where_ref, *refs):
    hs, ds, ls = refs[:count], refs[count : 2 * count], refs[2 * count : 3 * count]
    gains, gain_two, out_ref = refs[3 * count : 4 * count], refs[4 * count], refs[4 * count + 1]
    columns = ds[0].shape[1]
    lefts = [h[...].T for h in hs]
    for at in range(0, columns, 512):
        cols = slice(at, at + 512)
        total = mm(lefts[0], ds[0][:, cols])
        for i in range(1, count):
            total = total + mm(lefts[i], ds[i][:, cols])
        store_cores(where_ref, out_ref, cols, total.astype(BF16))
    small = mm_nt(lefts[0], ls[0][...])
    for i in range(1, count):
        small = small + mm_nt(lefts[i], ls[i][...])
    gain_one = gains[0][...]
    for i in range(1, count):
        gain_one = gain_one + gains[i][...]
    extra = ls[0].shape[0]
    width = gain_one.shape[1]
    line = lax.broadcasted_iota(jnp.int32, (extra, width), 0)
    rows = jnp.where(line == beta, gain_one, jnp.where(line == beta + 1, gain_two[...], 0.0))
    eye = lax.broadcasted_iota(jnp.int32, (extra, extra), 0) == lax.broadcasted_iota(
        jnp.int32, (extra, extra), 1
    )
    small = small + mm_tn(rows, eye.astype(BF16))
    store_cores(where_ref, out_ref, slice(columns, None), small.astype(BF16))


def attn_grads(where, normed, dprojected, dlogits, gains, gain_two, beta):
    rows, width = normed[0].shape
    columns = dprojected[0].shape[1]
    extra = dlogits[0].shape[0]
    count = len(normed)
    block = width // 4
    whole = lambda shape: pl.BlockSpec(shape, lambda i: (0, 0))
    return pl.pallas_call(
        functools.partial(attn_grad_kernel, count, beta),
        grid=(4,),
        in_specs=[pl.BlockSpec(memory_space=pltpu.SMEM)]
        + [pl.BlockSpec((rows, block), lambda i: (0, i))] * count
        + [whole((rows, columns))] * count
        + [whole((extra, rows))] * count
        + [pl.BlockSpec((1, block), lambda i: (0, i))] * (count + 1),
        out_specs=pl.BlockSpec((2, block // 2, columns + extra), lambda i: (0, i, 0)),
        out_shape=jax.ShapeDtypeStruct((2, width // 2, columns + extra), BF16),
        name="attn_grads",
        compiler_params=params(),
        cost_estimate=cost(14),
    )(where, *normed, *dprojected, *dlogits, *gains, gain_two)


def out_grad_kernel(pieces, where_ref, *refs):
    dm_ref, out_ref, att = refs[pieces:]

    @pl.when(pl.program_id(0) == 0)
    def _():
        gather_pieces(refs[:pieces], att, 4)

    total = mm_tn(dm_ref[...], att[...]).astype(BF16)
    rows, inner = out_ref.shape[3:]
    for c in range(2):
        for s in range(4):
            out_ref[jnp.where(where_ref[16] == c, 0, 1), 0, s] = total[
                c * rows : (c + 1) * rows, s * inner : (s + 1) * inner
            ]


def out_grads(where, pieces, dm):
    rows, width = dm.shape
    part, inner = pieces[0].shape
    block = width // 4
    return pl.pallas_call(
        functools.partial(out_grad_kernel, len(pieces)),
        grid_spec=pltpu.PrefetchScalarGridSpec(
            num_scalar_prefetch=1,
            grid=(4,),
            in_specs=[pl.BlockSpec((part, inner), lambda i, w: (0, 0))] * len(pieces)
            + [pl.BlockSpec((rows, block), lambda i, w: (0, i))],
            out_specs=pl.BlockSpec((2, 1, 4, block // 2, inner), lambda i, w: (0, w[i], 0, 0, 0)),
            scratch_shapes=[pltpu.VMEM((rows, 4 * inner), BF16)],
        ),
        out_shape=jax.ShapeDtypeStruct((2, 4, 4, block // 2, inner), BF16),
        name="out_grads",
        compiler_params=params(),
        cost_estimate=cost(5),
    )(where, *pieces, dm)


def block_out_kernel(where_ref, mid_ref, own_ref, recv_ref, out_ref):
    total = mid_ref[...] + own_ref[...] + recv_ref[...].astype(F32)
    out_ref[...] = total.astype(out_ref.dtype)


def block_out_rows(where, middle, own, recv):
    rows, width = middle.shape
    block = width // 4
    flat = pl.BlockSpec((rows, block), lambda i, w: (0, i))
    return pl.pallas_call(
        block_out_kernel,
        grid_spec=pltpu.PrefetchScalarGridSpec(
            num_scalar_prefetch=1,
            grid=(4,),
            in_specs=[flat] * 3,
            out_specs=pl.BlockSpec((rows, block), lambda i, w: (0, w[i])),
        ),
        out_shape=jax.ShapeDtypeStruct((rows, width), BF16),
        name="block_out",
        compiler_params=params(),
        cost_estimate=cost(4),
    )(where, middle, own, recv)


def input_grad_kernel(where_ref, x_ref, own_ref, recv_ref, dmid_ref, gain_ref, *refs):
    out_ref = refs[-1]
    rows = x_ref[...].astype(F32)
    scale = row_norm(rows)
    weighted = (own_ref[...].astype(F32) + recv_ref[...].astype(F32)) * gain_ref[...]
    inner = jnp.mean(rows * weighted, axis=-1, keepdims=True)
    out_ref[...] = scale * weighted - rows * (scale * scale * scale) * inner
    block = rows.shape[1] // 4
    for j in range(4):
        at = column(where_ref[j], block)
        out_ref[:, at] = out_ref[:, at] + dmid_ref[:, j * block : (j + 1) * block]


def input_grad_rows(where, rows_low, pieces, recv, dmiddle, gain, batch, total):
    _, part, width = pieces.shape
    own = pl.BlockSpec((None, part // 2, width), lambda i, w: (0, i, 0))
    flat = pl.BlockSpec((part // 2, width), lambda i, w: (i, 0))
    later = pl.BlockSpec((part // 2, width), lambda i, w: (i + 2 * batch, 0))
    first = total is None
    return pl.pallas_call(
        input_grad_kernel,
        grid_spec=pltpu.PrefetchScalarGridSpec(
            num_scalar_prefetch=1,
            grid=(2,),
            in_specs=[later, own, flat, later, pl.BlockSpec((1, width), lambda i, w: (0, 0))]
            + ([] if first else [pl.BlockSpec(memory_space=pl.ANY)]),
            out_specs=later,
        ),
        out_shape=jax.ShapeDtypeStruct(dmiddle.shape, F32),
        input_output_aliases={} if first else {6: 0},
        name="input_grad",
        compiler_params=params(),
        cost_estimate=cost(3),
    )(where, rows_low, pieces, recv, dmiddle, gain, *([] if first else [total]))


def product(left_side, right_side):
    return jnp.dot(left_side, right_side, preferred_element_type=F32)


def by_transposed(left_side, right_side):
    return lax.dot_general(
        left_side, right_side, (((1,), (1,)), ((), ())), preferred_element_type=F32
    )


def transposed_by(left_side, right_side):
    return lax.dot_general(
        left_side, right_side, (((0,), (0,)), ((), ())), preferred_element_type=F32
    )


def shift(values, axis, step):
    size = lax.axis_size(axis)
    return lax.ppermute(values, axis, [(i, (i + step) % size) for i in range(size)])


def ring_gather(values, axis):
    pieces = [values]
    for _ in range(lax.axis_size(axis) - 1):
        pieces.append(shift(pieces[-1], axis, 1))
    return pieces


def ring_scatter(pieces, axis):
    total = pieces[-1].astype(BF16)
    for piece in pieces[-2::-1]:
        total = shift(total, axis, -1).astype(F32) + piece.astype(F32)
        if piece is not pieces[0]:
            total = total.astype(BF16)
    return total


def row_scale(rows):
    return lax.rsqrt(jnp.mean(rows * rows, axis=-1, keepdims=True) + 1e-06)


def norm_back(rows, scale, gain, upstream):
    weighted = upstream * gain
    inner = jnp.mean(rows * weighted, axis=-1, keepdims=True)
    grad = scale * weighted - rows * (scale * scale * scale) * inner
    return grad, jnp.sum(upstream * rows * scale, axis=0)


def place(pieces, axis, order):
    size = lax.axis_size(axis)
    index = lax.axis_index(axis)
    height = pieces[0].shape[0]
    whole = jnp.zeros((size * height,) + pieces[0].shape[1:], pieces[0].dtype)
    for s, piece in enumerate(pieces):
        at = ((index + order * s) % size) * height
        whole = lax.dynamic_update_slice_in_dim(whole, piece, at, 0)
    return whole


def cut(whole, axis, step):
    size = lax.axis_size(axis)
    height = whole.shape[0] // size
    at = ((lax.axis_index(axis) + step) % size) * height
    return lax.dynamic_slice_in_dim(whole, at, height, 0)


def by_core(own, other, axis):
    first = lax.axis_index("core") == 0
    return jnp.where(
        first, jnp.concatenate([own, other], axis), jnp.concatenate([other, own], axis)
    )


def general_body(
    tokens,
    lengths,
    cotangent,
    q_weight,
    k_weight,
    v_weight,
    direction_weight,
    beta_weight,
    out_weight,
    gate_weight,
    up_weight,
    down_weight,
    norm_gain_one,
    norm_gain_two,
):
    zsize = lax.axis_size("head")
    core = lax.axis_index("core")
    plane = ("da", "db")
    dp = ("da", "db", "core")
    micro, slots, part, width = tokens.shape
    count = micro * slots
    local = count * part
    shard = q_weight.shape[0]
    heads = beta_weight.shape[1]
    inner = heads * HEAD_DIM
    half = gate_weight.shape[1] // 2
    rows_low = tokens.reshape(count, part, width)
    rows_in = rows_low.reshape(local, width).astype(F32)
    cot_own = cotangent.reshape(local, width)
    seq_lengths = lengths.reshape(count)

    sequences = [place(ring_gather(rows_low[i], "head"), "head", -1) for i in range(count)]

    small = jnp.concatenate(
        [beta_weight.T, norm_gain_one[None, :], norm_gain_two[None, :]], axis=0
    )
    small = lax.all_gather(small, dp, axis=1, tiled=True)
    beta_rows = small[:heads]
    gain_one = small[heads].astype(F32)
    gain_two = small[heads + 1].astype(F32)
    attn_local = jnp.stack(
        [w.reshape(shard, heads, HEAD_DIM) for w in (q_weight, k_weight, v_weight, direction_weight)],
        axis=2,
    ).reshape(shard, 4 * inner)
    attn_weight = lax.all_gather(attn_local, dp, axis=0, tiled=True)
    out_pieces = ring_gather(out_weight.T, "head")
    out_all = jnp.concatenate(out_pieces, axis=1)
    out_all = lax.all_gather(out_all, dp, axis=0, tiled=True)
    ffn_local = jnp.concatenate(
        [w.reshape(shard, 2, half) for w in (gate_weight, up_weight, down_weight.T)], axis=2
    )
    ffn_own = lax.dynamic_index_in_dim(ffn_local, core, 1, keepdims=False)
    ffn_other = lax.dynamic_index_in_dim(ffn_local, 1 - core, 1, keepdims=False)
    ffn_other = shift(ffn_other, "core", 1)
    ffn_chip = by_core(ffn_own, ffn_other, 0)
    ffn_weight = [
        lax.all_gather(w, plane, axis=0, tiled=True) for w in ring_gather(ffn_chip, "head")
    ]

    normed, projected, logits, kept, mixed = [], [], [], [], []
    for i in range(count):
        rows = sequences[i].astype(F32)
        h1 = (rows * row_scale(rows) * gain_one).astype(BF16)
        normed.append(h1)
        projected.append(product(h1, attn_weight).astype(BF16))
        logits.append(by_transposed(beta_rows, h1))
        result = attention_forward(None, seq_lengths[i : i + 1], projected[i], logits[i])
        kept.append(result[1:])
        pieces = [cut(result[0], "head", 0)]
        for s in range(1, zsize):
            pieces.append(shift(cut(result[0], "head", s), "head", s))
        mixed.append(jnp.concatenate(pieces, axis=1))
    attended = jnp.concatenate(mixed, axis=0)
    middle = rows_in + by_transposed(attended, out_all)
    scale_two = row_scale(middle)
    h2_own = (middle * scale_two * gain_two).astype(BF16)
    h2 = jnp.concatenate([h2_own, shift(h2_own, "core", 1)], axis=0)
    cot = jnp.concatenate([cot_own, shift(cot_own, "core", 1)], axis=0)

    out_sum = None
    dh2_sum = None
    ffn_terms = []
    for weight in ffn_weight:
        gate_up = product(h2, weight[:, : 2 * half])
        dhidden = product(cot, weight[:, 2 * half :])
        gate = gate_up[:, :half]
        up = gate_up[:, half:]
        sig = jax.nn.sigmoid(gate)
        hidden = (gate * sig * up).astype(BF16)
        dgate = (dhidden * up * sig * (1.0 + gate * (1.0 - sig))).astype(BF16)
        dup = (dhidden * gate * sig).astype(BF16)
        dgate_up = jnp.concatenate([dgate, dup], axis=1)
        out_part = by_transposed(hidden, weight[:, 2 * half :])
        dh2_part = by_transposed(dgate_up, weight[:, : 2 * half])
        out_sum = out_part if out_sum is None else out_sum + out_part
        dh2_sum = dh2_part if dh2_sum is None else dh2_sum + dh2_part
        ffn_terms.append(
            jnp.concatenate(
                [
                    transposed_by(h2, dgate_up).astype(BF16),
                    transposed_by(cot, hidden).astype(BF16),
                ],
                axis=1,
            )
        )
    dh2 = dh2_sum[:local] + shift(dh2_sum[local:].astype(BF16), "core", 1).astype(F32)
    down = out_sum[:local] + shift(out_sum[local:].astype(BF16), "core", 1).astype(F32)
    block_out = (middle + down).astype(BF16)
    dmid, gain_two_grad = norm_back(middle, scale_two, gain_two, dh2)
    dmiddle = cot_own.astype(F32) + dmid
    dm = dmiddle.astype(BF16)
    dattended = product(dm, out_all).astype(BF16)
    out_term = transposed_by(dm, attended).astype(BF16)

    attn_term = None
    beta_term = None
    dh1_parts = []
    for i in range(count):
        rows = dattended[i * part : (i + 1) * part]
        pieces = [rows[:, :inner]]
        for s in range(1, zsize):
            pieces.append(shift(rows[:, s * inner : (s + 1) * inner], "head", -s))
        grad_out = place(pieces, "head", 1)
        dprojected, dlogits = attention_backward(
            None, seq_lengths[i : i + 1], projected[i], logits[i], [grad_out[None]], 0, kept[i]
        )
        dlogits = dlogits.astype(BF16)
        dh1 = by_transposed(dprojected, attn_weight) + transposed_by(dlogits, beta_rows)
        dh1 = dh1.astype(BF16)
        dh1_parts.append(ring_scatter([cut(dh1, "head", -s) for s in range(zsize)], "head"))
        term = transposed_by(normed[i], dprojected)
        attn_term = term if attn_term is None else attn_term + term
        term = product(dlogits, normed[i])
        beta_term = term if beta_term is None else beta_term + term
    dh1 = jnp.concatenate(dh1_parts, axis=0)
    scale_one = row_scale(rows_in)
    drows, gain_one_grad = norm_back(rows_in, scale_one, gain_one, dh1)
    input_grad = dmiddle + drows

    ffn_total = ring_scatter(
        [lax.psum_scatter(t, plane, scatter_dimension=0, tiled=True) for t in ffn_terms], "head"
    )
    ffn_total = ffn_total.reshape(2, shard, 3 * half)
    own = lax.dynamic_index_in_dim(ffn_total, core, 0, keepdims=False)
    other = lax.dynamic_index_in_dim(ffn_total, 1 - core, 0, keepdims=False)
    other = shift(other.astype(BF16), "core", 1).astype(F32)
    gate_grad, up_grad, down_grad = [
        by_core(own[:, j * half : (j + 1) * half], other[:, j * half : (j + 1) * half], 1)
        for j in range(3)
    ]
    out_total = lax.psum_scatter(out_term, dp, scatter_dimension=0, tiled=True)
    out_total = ring_scatter(
        [out_total[:, s * inner : (s + 1) * inner] for s in range(zsize)], "head"
    )
    attn_total = lax.psum_scatter(attn_term.astype(BF16), dp, scatter_dimension=0, tiled=True)
    attn_total = attn_total.astype(F32).reshape(shard, heads, 4, HEAD_DIM)
    small_term = jnp.concatenate(
        [beta_term, gain_one_grad[None, :], gain_two_grad[None, :]], axis=0
    )
    small_total = lax.psum_scatter(small_term, dp, scatter_dimension=1, tiled=True)
    gain_grads = lax.psum(small_total[heads:], "head")
    shape = (micro, slots, part, width)
    return (
        block_out.reshape(shape),
        input_grad.reshape(shape),
        attn_total[:, :, 0].reshape(shard, inner),
        attn_total[:, :, 1].reshape(shard, inner),
        attn_total[:, :, 2].reshape(shard, inner),
        attn_total[:, :, 3].reshape(shard, inner),
        small_total[:heads].T,
        out_total.T,
        gate_grad,
        up_grad,
        down_grad.T,
        gain_grads[0],
        gain_grads[1],
    )


def after(values, others):
    return lax.optimization_barrier((values, others))[0]


def swap(values, axis, mask):
    size = lax.axis_size(axis)
    return lax.ppermute(values, axis, [(i, i ^ mask) for i in range(size)])


def plane_swap(values, mask):
    return lax.ppermute(values, ("da", "db"), [(i, i ^ mask) for i in range(4)])


class Plan:
    def __init__(self):
        self.made = {}
        self.waiting = []
        self.last = None

    def get(self, name):
        return self.made[name]

    def send(self, name, needs, start):
        self.waiting.append((name, needs, start))
        self.flush()

    def flush(self):
        progress = True
        while progress:
            progress = False
            for item in list(self.waiting):
                name, needs, start = item
                gates = PLAN["gates"].get(name, [])
                if all(need in self.made for need in list(needs) + list(gates)):
                    self.waiting.remove(item)
                    values = [self.made[need] for need in needs]
                    if gates:
                        values[0] = after(values[0], [self.made[gate] for gate in gates])
                    self.made[name] = start(*values)
                    progress = True

    def put(self, name, value):
        self.made[name] = value
        self.flush()

    def step(self, name, value, work):
        holds = [self.made[pin] for pin in PLAN["pins"].get(name, []) if pin in self.made]
        if self.last is not None:
            holds.append(self.last)
        result = work(after(value, holds) if holds else value)
        self.last = result[0] if isinstance(result, (tuple, list)) else result
        self.put(name, result)


def body(
    tokens,
    lengths,
    cotangent,
    q_weight,
    k_weight,
    v_weight,
    direction_weight,
    beta_weight,
    out_weight,
    gate_weight,
    up_weight,
    down_weight,
    norm_gain_one,
    norm_gain_two,
):
    plan = Plan()
    get, put, send, step = plan.get, plan.put, plan.send, plan.step
    core = lax.axis_index("core")
    z = lax.axis_index("head")
    plane_at = [
        (lax.axis_index("da") ^ a) * 2 + (lax.axis_index("db") ^ b)
        for a in range(2)
        for b in range(2)
    ]
    where = jnp.stack(
        plane_at
        + [(z - s) % 4 for s in range(4)]
        + [(z + s) % 4 for s in range(4)]
        + [(p - z) % 4 for p in range(4)]
        + [core]
    ).astype(jnp.int32)
    dp = ("da", "db", "core")
    micro, slots, part, width = tokens.shape
    count = micro * slots
    local = count * part
    shard = q_weight.shape[0]
    heads = beta_weight.shape[1]
    inner = heads * HEAD_DIM
    columns = 4 * inner
    half = gate_weight.shape[1] // 2
    rows_low = tokens.reshape(count, part, width)
    flat_low = rows_low.reshape(local, width)
    cot_own = cotangent.reshape(local, width)
    seq_lengths = lengths.reshape(count)
    ahead = lambda values: shift(values, "head", 1)
    back = lambda values: shift(values, "head", -1)

    attn_local = jnp.stack(
        [w.reshape(shard, heads, HEAD_DIM) for w in (q_weight, k_weight, v_weight, direction_weight)],
        axis=2,
    ).reshape(shard, columns)
    small = jnp.concatenate(
        [beta_weight, norm_gain_one[:, None], norm_gain_two[:, None]], axis=1
    )
    small = jnp.pad(small, ((0, 0), (0, 128 - small.shape[1])))
    put(ATTN_ROWS, jnp.concatenate([attn_local, small], axis=1))
    put(OUT_ROWS, out_weight.T)
    ffn_local = jnp.concatenate(
        [w.reshape(shard, 2, half) for w in (gate_weight, up_weight, down_weight.T)], axis=2
    )
    put(FFN_OWN, lax.dynamic_index_in_dim(ffn_local, core, 1, keepdims=False))
    put(FFN_GIVE, lax.dynamic_index_in_dim(ffn_local, 1 - core, 1, keepdims=False))
    put(COT, cot_own)

    send(ATTN, [ATTN_ROWS], lambda v: lax.all_gather(v, dp, axis=0, tiled=True))
    send(FFN_TAKE, [FFN_GIVE], lambda v: swap(v, "core", 1))
    send((HOP, 0), [FFN_TAKE, FFN_OWN], lambda take, own: by_core(own, take, 0))
    for i in range(count):
        put((TOK, i, 0), rows_low[i])
        for s in range(1, 4):
            send((TOK, i, s), [(TOK, i, s - 1)], ahead)
    for s in range(1, 4):
        send((HOP, s), [(HOP, s - 1)], ahead)
    for s in range(4):
        if s in PLAN["direct"]:
            for mask in range(1, 4):
                send((CHUNK, s, mask), [(HOP, s)], lambda v, mask=mask: plane_swap(v, mask))
        else:
            send(
                (CHUNK, s, 0),
                [(HOP, s)],
                lambda v: lax.all_gather(v, ("da", "db"), axis=0, tiled=True),
            )
    for s in range(1, 4):
        send((OUT, s), [OUT_ROWS], lambda v, s=s: shift(v, "head", s))
    send(
        OUT_ALL,
        [(OUT, 1), (OUT, 2), (OUT, 3)],
        lambda *v: lax.all_gather(
            jnp.concatenate([out_weight.T] + list(v), axis=0), dp, axis=0, tiled=True
        ),
    )
    send(COT_OTHER, [COT], lambda v: swap(v, "core", 1))

    def chunk(s):
        if s in PLAN["direct"]:
            return [get((HOP, s))] + [get((CHUNK, s, mask)) for mask in range(1, 4)]
        return [get((CHUNK, s, 0))]

    def small_rows():
        turned_small = get(ATTN)[:, columns:].T
        gains = [turned_small[heads + i : heads + i + 1].astype(F32) for i in range(2)]
        return turned_small[:8], gains[0], gains[1]

    def mixed():
        pieces = []
        for i in range(count):
            pieces += [get((ATTEND, i))[0][0]] + [get((MIX, i, s)) for s in range(1, 4)]
        return pieces

    def project_step(i):
        small8, gain_one, _ = small_rows()
        pieces = [get((TOK, i, s)) for s in range(1, 4)]
        step(
            (PROJECT, i),
            rows_low[i],
            lambda v: project(where, [v] + pieces, get(ATTN), small8, gain_one, columns)[::-1],
        )

    def forward_step(i):
        logit, packed, _ = get((PROJECT, i))
        step(
            (ATTEND, i),
            packed,
            lambda v: attention_forward(where, seq_lengths[i : i + 1], v, logit),
        )
        for s in range(1, 4):
            send((MIX, i, s), [(ATTEND, i)], lambda v, s=s: shift(v[0][s], "head", s))

    def turn_cot():
        step(
            TURN_COT, cot_own, lambda v: turned(where, v, get(COT_OTHER), True)
        )

    def middle_step():
        pieces = mixed()
        out_all = get(OUT_ALL).reshape(8, 4, shard, inner)
        _, _, gain_two = small_rows()
        step(
            MIDDLE,
            pieces[0],
            lambda v: middle_rows(where, [v] + pieces[1:], out_all, flat_low, gain_two)[::-1],
        )
        send(H2_OTHER, [MIDDLE], lambda v: swap(v[0], "core", 1))

    def feed_step(s):
        total = get((FEED, s - 1))[1] if s else None
        h2 = get(MIDDLE)[0]
        step(
            (FEED, s),
            h2,
            lambda v: feed_forward_part(
                where, (v, get(H2_OTHER)), get(TURN_COT)[:2], chunk(s), total, s == 3
            ),
        )
        if s == 3:
            send(DH_OTHER, [(FEED, 3)], lambda v: swap(v[2], "core", 1))

    def turn_h2():
        step(TURN_H2, get(MIDDLE)[0], lambda v: turned(where, v, get(H2_OTHER), False)[0])

    def grads(name, c, blocks, added):
        step(
            name,
            get((FEED, c))[0],
            lambda v: weight_grads(get(TURN_H2), get(TURN_COT)[2], v, blocks, added),
        )

    def far_step(c):
        if c in PLAN["whole"]:
            step(
                (GRAD_FAR, c),
                get((FEED, c))[0],
                lambda v: whole_weight_grads(where, get(TURN_H2), get(TURN_COT)[2], v),
            )
            send(
                (PLANE_SUM, c),
                [(GRAD_FAR, c)],
                lambda v: lax.psum_scatter(v, ("da", "db"), scatter_dimension=0, tiled=True),
            )
            if c == 1:
                send((SUM, c), [(PLANE_SUM, c)], ahead)
            else:
                send(
                    (SUM, c),
                    [(PLANE_SUM, c), (SUM, c - 1)],
                    lambda v, last: ahead((v.astype(F32) + last.astype(F32)).astype(BF16)),
                )
            return
        first = c in PLAN["da_first"]
        grads((GRAD_FAR, c), c, [2, 3] if first else [1, 3], [[], []])
        send((FAR, c), [(GRAD_FAR, c)], lambda v: swap(v, "da" if first else "db", 1))

    def middle_grads(c):
        if c in PLAN["whole"]:
            return
        first = c in PLAN["da_first"]
        grads((GRAD_MIDDLE, c), c, [1] if first else [2], [[(get((FAR, c)), 1)]])
        send((MID, c), [(GRAD_MIDDLE, c)], lambda v: swap(v, "db" if first else "da", 1))

    def near_terms(c):
        terms = [(get((FAR, c)), 0), (get((MID, c)), 0)]
        return terms + ([(get((SUM, (c - 1) % 4)), 0)] if c != 1 else [])

    def near_step(c):
        if c in PLAN["whole"]:
            return
        grads((GRAD_NEAR, c), c, [0], [near_terms(c)])
        send((SUM, c), [(GRAD_NEAR, c)], ahead)

    def last_step():
        step(
            LAST,
            get((FEED, 0))[0],
            lambda v: last_weight_grads(where, get(TURN_H2), get(TURN_COT)[2], v, near_terms(0)),
        )
        send(LAST_OTHER, [LAST], lambda v: swap(v[1], "core", 1))

    def norm_step():
        _, _, gain_two = small_rows()
        out_all = get(OUT_ALL).reshape(8, 4, shard, inner)
        step(
            NORM,
            get((FEED, 3))[1],
            lambda v: norm_two(
                where, v, get(DH_OTHER), get(MIDDLE)[1], get(TURN_COT)[0], gain_two, out_all, count
            ),
        )
        for s in range(1, 4):
            send((SENT, s), [NORM], lambda v, s=s: shift(v[2][s], "head", -s))

    def out_step():
        step(OUT_GRAD, get(NORM)[1], lambda v: out_grads(where, mixed(), v))
        send(OUT_CORE, [OUT_GRAD], lambda v: swap(v[1], "core", 1))
        send(
            OUT_RS,
            [OUT_GRAD, OUT_CORE],
            lambda v, other: lax.psum_scatter(
                (v[0].astype(F32) + other.astype(F32)).astype(BF16).reshape(16 * shard, inner),
                ("da", "db"),
                scatter_dimension=0,
                tiled=True,
            ),
        )
        for s in range(1, 4):
            send(
                (OUTSUM, s),
                [OUT_RS, (OUTSUM, s - 1)] if s > 1 else [OUT_RS],
                lambda v, *last, s=s: back(
                    (last[0].astype(F32) + v[(4 - s) * shard : (5 - s) * shard].astype(F32)).astype(
                        BF16
                    )
                    if last
                    else v[3 * shard :]
                ),
            )

    def down_step():
        chunks = [chunk(s) for s in range(4)]
        step(
            DOWN,
            get((FEED, 0))[0],
            lambda v: down_rows(
                where, [v] + [get((FEED, s))[0] for s in range(1, 4)], chunks, width
            ),
        )
        send(DOWN_OTHER, [DOWN], lambda v: swap(v[1], "core", 1))

    def backward_step(i):
        logit, packed, _ = get((PROJECT, i))
        sent = [get(NORM)[2][0]] + [get((SENT, s)) for s in range(1, 4)]
        step(
            (BACK, i),
            packed,
            lambda v: attention_backward(
                where, seq_lengths[i : i + 1], v, logit, sent, i, get((ATTEND, i))[1:]
            ),
        )

    def dh1_step(i):
        small8, gain_one, _ = small_rows()
        dpacked, dlogit = get((BACK, i))
        normed = get((PROJECT, i))[2]
        step(
            (DH, i),
            dpacked,
            lambda v: dh1_pieces(where, v, dlogit, normed, get(ATTN), small8, gain_one),
        )
        send((RING, i, 1), [(DH, i)], lambda v: back(v[0][3]))
        for s in (2, 3):
            send(
                (RING, i, s),
                [(RING, i, s - 1), (DH, i)],
                lambda v, d, s=s: back(
                    (v.astype(F32) + d[0][4 - s].astype(F32)).astype(BF16)
                ),
            )

    def attn_step():
        step(
            ATTN_GRAD,
            get((BACK, 0))[0],
            lambda v: attn_grads(
                where,
                [get((PROJECT, i))[2] for i in range(count)],
                [v] + [get((BACK, i))[0] for i in range(1, count)],
                [get((BACK, i))[1] for i in range(count)],
                [get((DH, i))[1] for i in range(count)],
                get(NORM)[3],
                heads,
            ),
        )
        send(ATTN_CORE, [ATTN_GRAD], lambda v: swap(v[1], "core", 1))
        send(
            ATTN_RS,
            [ATTN_GRAD, ATTN_CORE],
            lambda v, other: lax.psum_scatter(
                (v[0].astype(F32) + other.astype(F32)).astype(BF16),
                ("da", "db"),
                scatter_dimension=0,
                tiled=True,
            ).astype(F32),
        )
        send((GAIN, 0), [ATTN_RS], lambda v: v[:, columns + heads : columns + heads + 2].T)
        send((GAIN, 1), [(GAIN, 0)], lambda v: v + swap(v, "head", 1))
        send((GAIN, 2), [(GAIN, 1)], lambda v: v + swap(v, "head", 2))

    def input_step(i):
        _, gain_one, _ = small_rows()
        total = get((INPUT, 0)) if i else None
        step(
            (INPUT, i),
            get(NORM)[0],
            lambda v: input_grad_rows(
                where, flat_low, get((DH, i))[0], get((RING, i, 3)), v, gain_one, i, total
            ),
        )

    def block_step():
        step(
            BLOCK_OUT,
            get(MIDDLE)[1],
            lambda v: block_out_rows(where, v, get(DOWN)[0], get(DOWN_OTHER)),
        )

    def finish_step():
        step(FINISH, get(LAST)[0], lambda v: finish_grads(where, v, get(LAST_OTHER)))

    steps = {TURN_COT: turn_cot, MIDDLE: middle_step, TURN_H2: turn_h2, NORM: norm_step, OUT_GRAD: out_step}
    steps |= {DOWN: down_step, ATTN_GRAD: attn_step, BLOCK_OUT: block_step, LAST: last_step}
    steps[FINISH] = finish_step
    for i in range(2):
        steps[(PROJECT, i)] = functools.partial(project_step, i)
        steps[(ATTEND, i)] = functools.partial(forward_step, i)
        steps[(BACK, i)] = functools.partial(backward_step, i)
        steps[(DH, i)] = functools.partial(dh1_step, i)
        steps[(INPUT, i)] = functools.partial(input_step, i)
    for c in range(4):
        steps[(FEED, c)] = functools.partial(feed_step, c)
        steps[(GRAD_FAR, c)] = functools.partial(far_step, c)
        steps[(GRAD_MIDDLE, c)] = functools.partial(middle_grads, c)
        if c:
            steps[(GRAD_NEAR, c)] = functools.partial(near_step, c)
    for name in PLAN["order"]:
        steps[name]()

    attn_total = get(ATTN_RS)
    beta_grad = attn_total[:, columns : columns + heads]
    attn_total = attn_total[:, :columns].reshape(shard, heads, 4, HEAD_DIM)
    gate_grad, up_grad, down_grad = get(FINISH)
    gains = get((GAIN, 2))
    shape = (micro, slots, part, width)
    return (
        get(BLOCK_OUT).reshape(shape),
        get((INPUT, 1)).reshape(shape),
        attn_total[:, :, 0].reshape(shard, inner),
        attn_total[:, :, 1].reshape(shard, inner),
        attn_total[:, :, 2].reshape(shard, inner),
        attn_total[:, :, 3].reshape(shard, inner),
        beta_grad,
        (get(OUT_RS)[:shard].astype(F32) + get((OUTSUM, 3)).astype(F32)).T,
        gate_grad,
        up_grad,
        down_grad.T,
        gains[0],
        gains[1],
    )


def solution(mesh):
    dp_size = mesh.shape["dp"]
    fine = Mesh(
        mesh.devices.reshape(dp_size // 4, 2, 2, mesh.shape["head"]), ("da", "db", "core", "head")
    )
    dp = ("da", "db", "core")
    rows = P(None, dp, "head", None)
    wide = P(dp, "head")
    tall = P("head", dp)
    in_specs = (
        rows, P(None, dp), rows, wide, wide, wide, wide, wide, tall, wide, wide, tall, P(dp), P(dp)
    )
    out_specs = (rows, rows, wide, wide, wide, wide, wide, tall, wide, wide, tall, P(dp), P(dp))
    special = dp_size == 8 and mesh.shape["head"] == 4
    return jax.shard_map(
        body if special else general_body,
        mesh=fine,
        in_specs=in_specs,
        out_specs=out_specs,
        check_vma=False,
    )
```

```python
import functools

import jax
import jax.numpy as jnp
from jax import lax
from jax.experimental import pallas as pl
from jax.experimental.pallas import tpu as pltpu
from jax.sharding import Mesh, PartitionSpec as P

HEAD_DIM = 128
TILE = 128
F32 = jnp.float32
BF16 = jnp.bfloat16
COST_SCALE = 2.5e+09
(
    ATTN_ROWS,
    OUT_ROWS,
    FFN_OWN,
    FFN_GIVE,
    COT,
    ATTN,
    FFN_TAKE,
    HOP,
    TOK,
    CHUNK,
    OUT,
    OUT_ALL,
    COT_OTHER,
    ATTEND,
    MIX,
    PROJECT,
    TURN_COT,
    MIDDLE,
    H2_OTHER,
    FEED,
    DH_OTHER,
    TURN_H2,
    GRAD_FAR,
    PLANE_SUM,
    SUM,
    FAR,
    GRAD_MIDDLE,
    MID,
    GRAD_NEAR,
    LAST,
    LAST_OTHER,
    NORM,
    SENT,
    OUT_GRAD,
    OUT_CORE,
    OUT_RS,
    OUTSUM,
    DOWN,
    DOWN_OTHER,
    BACK,
    DH,
    RING,
    ATTN_GRAD,
    ATTN_CORE,
    ATTN_RS,
    GAIN,
    INPUT,
    BLOCK_OUT,
    FINISH,
) = range(49)
PLAN = {
    "order": (
        (PROJECT, 0),
        (ATTEND, 0),
        TURN_COT,
        (PROJECT, 1),
        (ATTEND, 1),
        MIDDLE,
        (FEED, 0),
        TURN_H2,
        (FEED, 1),
        (GRAD_FAR, 1),
        (FEED, 2),
        (GRAD_FAR, 2),
        (FEED, 3),
        NORM,
        (GRAD_FAR, 3),
        OUT_GRAD,
        (BACK, 0),
        (DH, 0),
        DOWN,
        (GRAD_FAR, 0),
        (BACK, 1),
        (DH, 1),
        ATTN_GRAD,
        (GRAD_MIDDLE, 0),
        (INPUT, 0),
        BLOCK_OUT,
        LAST,
        (INPUT, 1),
        FINISH,
    ),
    "direct": (2,),
    "da_first": (0,),
    "whole": (1, 2, 3),
    "gates": {
        (TOK, 1, 3): ((ATTEND, 0),),
        (HOP, 1): ((TOK, 1, 3),),
        (HOP, 2): ((PROJECT, 1),),
        (HOP, 3): ((ATTEND, 1),),
        (CHUNK, 0, 0): (ATTN_ROWS,),
        OUT_ALL: (TURN_COT,),
        (CHUNK, 3, 0): (MIDDLE,),
        (TOK, 0, 2): ((HOP, 0),),
        (OUT, 1): ((TOK, 1, 3),),
        (OUT, 2): ((TOK, 1, 3),),
        (OUT, 3): ((TOK, 1, 3),),
        (CHUNK, 1, 0): ((ATTEND, 1),),
        OUT_RS: ((GRAD_FAR, 0),),
    },
    "pins": {
        (ATTEND, 1): ((CHUNK, 0, 0),),
        (GRAD_FAR, 0): ((RING, 0, 1),),
        (DH, 0): ((SUM, 1),),
        (FEED, 1): ((MIX, 1, 1),),
        (DH, 1): ((RING, 0, 2),),
        ATTN_GRAD: ((RING, 0, 3),),
        (GRAD_MIDDLE, 0): ((RING, 1, 1), (SUM, 2)),
    },
}
QUERY, KEY, VALUE, RAW = [slice(i * HEAD_DIM, (i + 1) * HEAD_DIM) for i in range(4)]


def mm(left, right):
    return lax.dot_general(
        left.astype(BF16), right.astype(BF16), (((1,), (0,)), ((), ())), preferred_element_type=F32
    )


def mm_nt(left, right):
    return lax.dot_general(
        left.astype(BF16), right.astype(BF16), (((1,), (1,)), ((), ())), preferred_element_type=F32
    )


def mm_tn(left, right):
    return lax.dot_general(
        left.astype(BF16), right.astype(BF16), (((0,), (0,)), ((), ())), preferred_element_type=F32
    )


def tile_index():
    rows = lax.broadcasted_iota(jnp.int32, (TILE, TILE), 0)
    cols = lax.broadcasted_iota(jnp.int32, (TILE, TILE), 1)
    return rows, cols


def each(function, *lists):
    return [function(*items) for items in zip(*lists)]


def unit_directions(raw):
    raw = raw.astype(F32)
    inv_norm = lax.rsqrt(jnp.sum(raw * raw, axis=-1, keepdims=True) + 1e-06)
    return raw * inv_norm, inv_norm


def get_row(ref, row, cols):
    block = ref[:, cols]
    lines = lax.broadcasted_iota(jnp.int32, block.shape, 0)
    return jnp.sum(jnp.where(lines == row, block, 0.0), axis=0, keepdims=True)


def set_row(ref, row, cols, value):
    block = ref[:, cols]
    lines = lax.broadcasted_iota(jnp.int32, block.shape, 0)
    ref[:, cols] = jnp.where(lines == row, value, block)


def inverse_tiles(lower):
    rows, cols = tile_index()
    identity = (rows == cols).astype(F32)
    width = 8
    part = (rows // width == cols // width).astype(F32)
    power = each(lambda a: a * part, lower)
    result = each(lambda a: identity - a, power)
    reach = 2
    while reach < width:
        power = each(lambda a: mm(a, a), power)
        result = each(lambda a, b: a + mm(a, b), result, power)
        reach *= 2
    while width < TILE:
        corner = (
            (rows // (2 * width) == cols // (2 * width)) & (rows // width != cols // width)
        ).astype(F32)
        inner = each(lambda a, b: mm(a * corner, b), lower, result)
        result = each(lambda a, b: a - mm(a, b), result, inner)
        width *= 2
    return result


def forward_kernel(
    where_ref, length_ref, x_ref, logit_ref,
    out_ref, tt_ref, e_ref, g_ref, d_ref, mq_ref, state_ref, prob_ref,
    mk_ref, local_ref, run_ref,
):
    seq_len = x_ref.shape[0]
    tiles = seq_len // TILE
    length = length_ref[0]
    head = pl.program_id(0)
    rows, cols = tile_index()
    below = (rows > cols).astype(F32)
    upto = (rows >= cols).astype(F32)
    span = [pl.ds(n * TILE, TILE) for n in range(tiles)]
    group = min(tiles, 8)
    for first in range(0, tiles, group):
        part = list(range(first, first + group))
        units = [unit_directions(x_ref[span[n], RAW])[0].astype(BF16) for n in part]
        queries = [x_ref[span[n], QUERY] for n in part]
        keys = [x_ref[span[n], KEY] for n in part]
        position = lax.broadcasted_iota(jnp.int32, (1, TILE), 1)
        strength = [
            jnp.where(
                position + n * TILE < length,
                jax.nn.sigmoid(get_row(logit_ref, head, slice(n * TILE, (n + 1) * TILE))),
                0.0,
            )
            for n in part
        ]
        gram = each(lambda w: mm_nt(w, w) * below, units)
        inverse = inverse_tiles(each(lambda g, b: g * b, gram, strength))
        turned = each(lambda t: t.T, inverse)
        for n, t in zip(part, turned):
            tt_ref[span[n], :] = t.astype(BF16)
        upper = each(lambda t, b: (t * b).astype(BF16), turned, strength)
        cross = each(lambda w, k: (mm_nt(w, k) * below).astype(BF16), units, keys)
        seen = each(lambda q, w: (mm_nt(q, w) * upto).astype(BF16), queries, units)
        weight = each(lambda a, u: mm_nt(a, u).astype(BF16), seen, upper)
        slope = each(lambda u, w: mm(u, w).astype(BF16), upper, units)
        moved_q = each(lambda q, e, w: (q.astype(F32) - mm(e, w)).astype(BF16), queries, weight, units)
        local = each(lambda q, k, e, c: mm_nt(q, k) - mm(e, c), queries, keys, weight, cross)
        moved_k = each(lambda k, c, g: k.astype(F32) - mm_tn(c, g), keys, cross, slope)
        step = each(lambda w, g: mm_tn(w, g).astype(BF16), units, slope)
        for i, n in enumerate(part):
            e_ref[span[n], :] = weight[i]
            g_ref[span[n], :] = slope[i]
            d_ref[span[n], :] = step[i]
            mq_ref[span[n], :] = moved_q[i]
            local_ref[span[n], :] = local[i]
            mk_ref[span[n], :] = moved_k[i]
    scale = HEAD_DIM ** (-0.5)
    offset = 0
    for n in range(tiles):
        done = n * TILE
        if n:
            old = pl.ds(0, done)
            past = run_ref[old, :]
            past_low = past.astype(BF16)
            state_ref[pl.ds(offset, done), :] = past_low
            offset += done
            scores = jnp.concatenate(
                [mm_nt(mq_ref[span[n], :], past_low), local_ref[span[n], :]], axis=1
            )
            if n + 1 < tiles:
                run_ref[old, :] = past - mm(past_low, d_ref[span[n], :])
        else:
            scores = local_ref[span[n], :]
        if n + 1 < tiles:
            run_ref[span[n], :] = mk_ref[span[n], :]
        wide = done + TILE
        row_at = lax.broadcasted_iota(jnp.int32, (TILE, wide), 0) + done
        col_at = lax.broadcasted_iota(jnp.int32, (TILE, wide), 1)
        allowed = (col_at <= row_at) & (col_at < length)
        scores = jnp.where(allowed, scores * scale, -1e30)
        top = jnp.max(scores, axis=-1, keepdims=True)
        weights = jnp.exp(scores - top)
        weights = weights * (1.0 / jnp.sum(weights, axis=-1, keepdims=True))
        weights = weights.astype(BF16)
        prob_ref[0, span[n], pl.ds(0, wide)] = weights
        mixed = mm(weights, x_ref[pl.ds(0, wide), VALUE]).astype(out_ref.dtype)
        if len(out_ref.shape) == 2:
            out_ref[span[n], :] = mixed
        else:
            per = out_ref.shape[1] // TILE
            row = (n % per) * TILE
            out_ref[where_ref[12 + n // per], row : row + TILE, :] = mixed


def backward_kernel(
    grad_count, where_ref, length_ref, x_ref, logit_ref, *refs
):
    grad_refs, refs = refs[:grad_count], refs[grad_count:]
    (
    tt_ref, e_ref, g_ref, d_ref, mq_ref, state_ref, prob_ref,
    dx_ref, dlogit_ref,
    run_ref, value_ref, dmq_ref, dlocal_ref, dmk_ref, dstep_ref, do_ref,
    ) = refs
    part = grad_refs[0].shape[0]

    @pl.when(pl.program_id(0) == 0)
    def _():
        dlogit_ref[...] = jnp.zeros_like(dlogit_ref)

    for s, ref in enumerate(grad_refs):
        at = where_ref[8 + s] * part if grad_count > 1 else 0
        do_ref[pl.ds(pl.multiple_of(at, TILE), part), :] = ref[...]
    seq_len = x_ref.shape[0]
    tiles = seq_len // TILE
    length = length_ref[0]
    head = pl.program_id(0)
    rows, cols = tile_index()
    below = (rows > cols).astype(F32)
    upto = (rows >= cols).astype(F32)
    identity = (rows == cols).astype(F32)
    scale = HEAD_DIM ** (-0.5)
    span = [pl.ds(n * TILE, TILE) for n in range(tiles)]
    offset = TILE * (tiles * (tiles - 1) // 2)
    for n in reversed(range(tiles)):
        done = n * TILE
        wide = done + TILE
        old = pl.ds(0, done)
        grad_out = do_ref[span[n], :]
        weights = prob_ref[0, span[n], pl.ds(0, wide)]
        grad_w = mm_nt(grad_out, x_ref[pl.ds(0, wide), VALUE])
        weights_full = weights.astype(F32)
        mixed = weights_full * grad_w
        total = jnp.sum(mixed, axis=-1, keepdims=True)
        grad_s = ((mixed - weights_full * total) * scale).astype(BF16)
        back = mm_tn(weights, grad_out)
        if n + 1 < tiles:
            value_ref[pl.ds(0, wide), :] = value_ref[pl.ds(0, wide), :] + back
        else:
            value_ref[...] = back
        dlocal_ref[span[n], :] = grad_s[:, done:]
        if n + 1 < tiles:
            dmk_ref[span[n], :] = run_ref[span[n], :].astype(BF16)
        else:
            dmk_ref[span[n], :] = jnp.zeros((TILE, HEAD_DIM), BF16)
        if n:
            offset -= done
            past = state_ref[pl.ds(offset, done), :]
            grad_far = grad_s[:, :done]
            dmq_ref[span[n], :] = mm(grad_far, past).astype(BF16)
            fresh = mm_tn(grad_far, mq_ref[span[n], :])
            if n + 1 < tiles:
                carried = run_ref[old, :]
                carried_low = carried.astype(BF16)
                dstep_ref[span[n], :] = (-mm_tn(past, carried_low)).astype(BF16)
                run_ref[old, :] = carried - mm_nt(carried_low, d_ref[span[n], :]) + fresh
            else:
                dstep_ref[span[n], :] = jnp.zeros((TILE, HEAD_DIM), BF16)
                run_ref[old, :] = fresh
        else:
            dmq_ref[span[n], :] = jnp.zeros((TILE, HEAD_DIM), BF16)
            dstep_ref[span[n], :] = jnp.zeros((TILE, HEAD_DIM), BF16)
    dx_ref[:, VALUE] = value_ref[...].astype(dx_ref.dtype)
    group = min(tiles, 8)
    for first in range(0, tiles, group):
        part = list(range(first, first + group))
        pairs = [unit_directions(x_ref[span[n], RAW]) for n in part]
        units = [p[0].astype(BF16) for p in pairs]
        queries = [x_ref[span[n], QUERY] for n in part]
        keys = [x_ref[span[n], KEY] for n in part]
        position = lax.broadcasted_iota(jnp.int32, (1, TILE), 1)
        gates = [
            jax.nn.sigmoid(get_row(logit_ref, head, slice(n * TILE, (n + 1) * TILE))) for n in part
        ]
        live = [(position + n * TILE < length).astype(F32) for n in part]
        strength = each(lambda s, m: s * m, gates, live)
        turned = [tt_ref[span[n], :] for n in part]
        weight = [e_ref[span[n], :] for n in part]
        slope = [g_ref[span[n], :] for n in part]
        dlocal = [dlocal_ref[span[n], :] for n in part]
        dmq = [dmq_ref[span[n], :] for n in part]
        dmk = [dmk_ref[span[n], :] for n in part]
        dstep = [dstep_ref[span[n], :] for n in part]
        gram = each(lambda w: mm_nt(w, w) * below, units)
        cross = each(lambda w, k: (mm_nt(w, k) * below).astype(BF16), units, keys)
        seen = each(lambda q, w: (mm_nt(q, w) * upto).astype(BF16), queries, units)
        upper = each(lambda t, b: (t.astype(F32) * b).astype(BF16), turned, strength)
        dweight = each(
            lambda dm, w, dl, c: (-(mm_nt(dm, w) + mm_nt(dl, c))).astype(BF16),
            dmq, units, dlocal, cross,
        )
        dcross = each(
            lambda e, dl, g, dm: ((-(mm_tn(e, dl) + mm_nt(g, dm))) * below).astype(BF16),
            weight, dlocal, slope, dmk,
        )
        dslope = each(
            lambda w, ds, c, dm: (mm(w, ds) - mm(c, dm)).astype(BF16), units, dstep, cross, dmk
        )
        dinv = each(
            lambda a, de, w, dg: (mm_tn(a, de) + mm_nt(w, dg)).astype(BF16),
            seen, dweight, units, dslope,
        )
        dseen = each(lambda de, u: (mm(de, u) * upto).astype(BF16), dweight, upper)
        inner = each(lambda d, t: mm(d, t), dinv, turned)
        dlower = each(lambda u, h: -mm(u, h) * below, upper, inner)
        dgram = each(lambda d, b: (d * b).astype(BF16), dlower, strength)
        dunit = each(
            lambda e, dm, g, ds, u, dg: mm_nt(g, ds) - mm_tn(e, dm) + mm_tn(u, dg),
            weight, dmq, slope, dstep, upper, dslope,
        )
        dunit = each(
            lambda acc, da, q, dc, k, dg, w: acc
            + mm_tn(da, q) + mm(dc, k) + mm(dg, w) + mm_tn(dg, w),
            dunit, dseen, queries, dcross, keys, dgram, units,
        )
        for i, n in enumerate(part):
            dx_ref[span[n], QUERY] = (
                dmq[i].astype(F32) + mm(dlocal[i], keys[i]) + mm(dseen[i], units[i])
            ).astype(dx_ref.dtype)
            dx_ref[span[n], KEY] = (
                dmk[i].astype(F32) + mm_tn(dlocal[i], queries[i]) + mm_tn(dcross[i], units[i])
            ).astype(dx_ref.dtype)
            raw = x_ref[span[n], RAW].astype(F32)
            inv_norm = pairs[i][1]
            along = jnp.sum(raw * dunit[i], axis=-1, keepdims=True)
            dx_ref[span[n], RAW] = (
                inv_norm * dunit[i] - raw * (inv_norm * inv_norm * inv_norm) * along
            ).astype(dx_ref.dtype)
            dstrength = jnp.sum(
                identity * inner[i] + dlower[i] * gram[i], axis=0, keepdims=True
            )
            set_row(
                dlogit_ref,
                head,
                slice(n * TILE, (n + 1) * TILE),
                dstrength * gates[i] * (1.0 - gates[i]) * live[i],
            )


def saved_shapes(heads, seq_len):
    tiles = seq_len // TILE
    flat = jax.ShapeDtypeStruct((seq_len, heads * HEAD_DIM), BF16)
    state = jax.ShapeDtypeStruct((TILE * max(1, tiles * (tiles - 1) // 2), heads * HEAD_DIM), BF16)
    prob = jax.ShapeDtypeStruct((heads, seq_len, seq_len), BF16)
    return [flat] * 5 + [state, prob]


def saved_specs(heads, seq_len):
    tiles = seq_len // TILE
    flat = pl.BlockSpec((seq_len, HEAD_DIM), lambda h: (0, h))
    state = pl.BlockSpec((TILE * max(1, tiles * (tiles - 1) // 2), HEAD_DIM), lambda h: (0, h))
    prob = pl.BlockSpec((1, seq_len, seq_len), lambda h: (h, 0, 0))
    return [flat] * 5 + [state, prob]


def packed_spec(seq_len):
    return pl.BlockSpec((seq_len, 4 * HEAD_DIM), lambda h: (0, h))


def attention_forward(where, length, projected, logits):
    seq_len = projected.shape[0]
    heads = projected.shape[1] // (4 * HEAD_DIM)
    flat = pl.BlockSpec((seq_len, HEAD_DIM), lambda h: (0, h))
    return pl.pallas_call(
        forward_kernel,
        grid=(heads,),
        in_specs=[pl.BlockSpec(memory_space=pltpu.SMEM)] * 2
        + [packed_spec(seq_len)]
        + [pl.BlockSpec(logits.shape, lambda h: (0, 0))],
        out_specs=[
            flat
            if where is None
            else pl.BlockSpec((4, seq_len // 4, HEAD_DIM), lambda h: (0, 0, h))
        ]
        + saved_specs(heads, seq_len),
        out_shape=[
            jax.ShapeDtypeStruct(
                (seq_len, heads * HEAD_DIM)
                if where is None
                else (4, seq_len // 4, heads * HEAD_DIM),
                BF16,
            )
        ]
        + saved_shapes(heads, seq_len),
        scratch_shapes=[
            pltpu.VMEM((seq_len, HEAD_DIM), F32),
            pltpu.VMEM((seq_len, TILE), F32),
            pltpu.VMEM((seq_len, HEAD_DIM), F32),
        ],
        name="attention_forward",
        compiler_params=pltpu.CompilerParams(vmem_limit_bytes=56 * 1024 * 1024),
        cost_estimate=cost(21),
    )(length if where is None else where, length, projected, logits)


def attention_backward(where, length, projected, logits, grad_out, batch, saved):
    seq_len = projected.shape[0]
    heads = projected.shape[1] // (4 * HEAD_DIM)
    flat = pl.BlockSpec((seq_len, HEAD_DIM), lambda h: (0, h))
    row = pl.BlockSpec(logits.shape, lambda h: (0, 0))
    result = pl.pallas_call(
        functools.partial(backward_kernel, len(grad_out)),
        grid=(heads,),
        in_specs=[pl.BlockSpec(memory_space=pltpu.SMEM)] * 2
        + [packed_spec(seq_len), row]
        + [pl.BlockSpec((None, seq_len // len(grad_out), HEAD_DIM), lambda h: (batch, 0, h))]
        * len(grad_out)
        + saved_specs(heads, seq_len),
        out_specs=[packed_spec(seq_len), row],
        out_shape=[
            jax.ShapeDtypeStruct(projected.shape, BF16),
            jax.ShapeDtypeStruct(logits.shape, F32),
        ],
        scratch_shapes=[
            pltpu.VMEM((seq_len, HEAD_DIM), F32),
            pltpu.VMEM((seq_len, HEAD_DIM), F32),
            pltpu.VMEM((seq_len, HEAD_DIM), BF16),
            pltpu.VMEM((seq_len, TILE), BF16),
            pltpu.VMEM((seq_len, HEAD_DIM), BF16),
            pltpu.VMEM((seq_len, HEAD_DIM), BF16),
            pltpu.VMEM((seq_len, HEAD_DIM), BF16),
        ],
        name="attention_backward",
        compiler_params=pltpu.CompilerParams(vmem_limit_bytes=56 * 1024 * 1024),
        cost_estimate=cost(22),
    )(
        length if where is None else where,
        length,
        projected,
        logits,
        *grad_out,
        *saved,
    )
    return result[0], result[1]


def cost(microseconds):
    return pl.CostEstimate(
        flops=int(microseconds * COST_SCALE), bytes_accessed=1, transcendentals=0
    )


def params(mebibytes=56):
    return pltpu.CompilerParams(vmem_limit_bytes=mebibytes * 1024 * 1024)


def column(index, width):
    return pl.ds(pl.multiple_of(index * width, 128), width)


def row_norm(rows):
    return lax.rsqrt(jnp.mean(rows * rows, axis=-1, keepdims=True) + 1e-06)


def project_kernel(where_ref, p0, p1, p2, p3, w_ref, small_ref, gain_ref, h_ref, out_ref, logit_ref):
    def work(piece):
        rows = piece[...].astype(F32)
        normed = (rows * row_norm(rows) * gain_ref[...]).astype(BF16)
        h_ref[...] = normed
        for at in range(0, out_ref.shape[1], 512):
            out_ref[:, at : at + 512] = mm(normed, w_ref[:, at : at + 512]).astype(BF16)
        logit_ref[...] = mm_nt(small_ref[...], normed)

    for s, piece in enumerate((p0, p1, p2, p3)):
        pl.when(pl.program_id(0) == s)(functools.partial(work, piece))


def project(where, pieces, weight, small, gain, columns):
    part, width = pieces[0].shape
    rows = part * len(pieces)
    whole = lambda shape: pl.BlockSpec(shape, lambda i, w: (0, 0))
    return pl.pallas_call(
        project_kernel,
        grid_spec=pltpu.PrefetchScalarGridSpec(
            num_scalar_prefetch=1,
            grid=(len(pieces),),
            in_specs=[whole((part, width))] * 4
            + [whole(weight.shape), whole(small.shape), whole((1, width))],
            out_specs=[
                pl.BlockSpec((part, width), lambda i, w: (w[4 + i], 0)),
                pl.BlockSpec((part, columns), lambda i, w: (w[4 + i], 0)),
                pl.BlockSpec((small.shape[0], part), lambda i, w: (0, w[4 + i])),
            ],
        ),
        out_shape=[
            jax.ShapeDtypeStruct((rows, width), BF16),
            jax.ShapeDtypeStruct((rows, columns), BF16),
            jax.ShapeDtypeStruct((small.shape[0], rows), F32),
        ],
        name="project_rows",
        compiler_params=params(),
        cost_estimate=cost(0.0027),
    )(where, *pieces, weight, small, gain)


def turn_kernel(where_ref, own_ref, other_ref, a_ref, b_ref, t_ref):
    own, other = own_ref[...], other_ref[...]
    a_ref[...] = own
    b_ref[...] = other
    rows = own.shape[0]
    t_ref[:, :rows] = own.T
    t_ref[:, rows:] = other.T


def turn_only_kernel(where_ref, own_ref, other_ref, t_ref):
    rows = own_ref.shape[0]
    t_ref[:, :rows] = own_ref[...].T
    t_ref[:, rows:] = other_ref[...].T


def turned(where, own, other, reorder):
    rows, width = own.shape
    block = width // 4
    place_in = (lambda i, w: (0, w[i])) if reorder else (lambda i, w: (0, i))
    flat = pl.BlockSpec((rows, block), lambda i, w: (0, i))
    tall = pl.BlockSpec((block, 2 * rows), lambda i, w: (i, 0))
    tall_shape = jax.ShapeDtypeStruct((width, 2 * rows), BF16)
    same = jax.ShapeDtypeStruct((rows, width), BF16)
    return pl.pallas_call(
        turn_kernel if reorder else turn_only_kernel,
        grid_spec=pltpu.PrefetchScalarGridSpec(
            num_scalar_prefetch=1,
            grid=(4,),
            in_specs=[pl.BlockSpec((rows, block), place_in)] * 2,
            out_specs=[flat, flat, tall] if reorder else [tall],
        ),
        out_shape=[same, same, tall_shape] if reorder else [tall_shape],
        name="turn_rows",
        compiler_params=params(),
        cost_estimate=cost(0.3),
    )(where, own, other)


def gather_pieces(refs, scratch, count):
    part, inner = refs[0].shape
    for i, ref in enumerate(refs):
        batch, s = i // count, i % count
        scratch[batch * part : (batch + 1) * part, s * inner : (s + 1) * inner] = ref[...]


def assemble(where_ref, block_ref, scratch):
    rows, inner = block_ref.shape[2:]
    for c in range(2):
        for s in range(4):
            scratch[c * rows : (c + 1) * rows, s * inner : (s + 1) * inner] = block_ref[c, s]


def middle_kernel(pieces, where_ref, *refs):
    att_refs = refs[:pieces]
    w_ref, x_ref, gain_ref, mid_ref, h_ref, att, total, gains, weight = refs[pieces:]
    step = pl.program_id(0)

    @pl.when(step == 0)
    def _():
        gather_pieces(att_refs, att, 4)
        total[...] = jnp.zeros_like(total)

    assemble(where_ref, w_ref, weight)
    block = weight.shape[0]
    mid = x_ref[...].astype(F32) + mm_nt(att[...], weight[...])
    at = column(step, block)
    mid_ref[:, at] = mid
    gains[:, at] = jnp.broadcast_to(gain_ref[...], (8, block))
    total[...] += jnp.broadcast_to(jnp.sum(mid * mid, axis=-1, keepdims=True), total.shape)

    @pl.when(step == 3)
    def _():
        scale = lax.rsqrt(total[:, :1] * (1.0 / (4 * block)) + 1e-06)
        h_ref[...] = (mid_ref[...] * scale * gains[:1, :]).astype(BF16)


def middle_rows(where, pieces, out_all, rows_low, gain):
    rows, width = rows_low.shape
    block = width // 4
    part, inner = pieces[0].shape
    full = pl.BlockSpec((rows, width), lambda i, w: (0, 0))
    return pl.pallas_call(
        functools.partial(middle_kernel, len(pieces)),
        grid_spec=pltpu.PrefetchScalarGridSpec(
            num_scalar_prefetch=1,
            grid=(4,),
            in_specs=[pl.BlockSpec((part, inner), lambda i, w: (0, 0))] * len(pieces)
            + [
                pl.BlockSpec((2,) + out_all.shape[1:], lambda i, w: (w[i], 0, 0, 0)),
                pl.BlockSpec((rows, block), lambda i, w: (0, w[i])),
                pl.BlockSpec((1, block), lambda i, w: (0, w[i])),
            ],
            out_specs=[full, full],
            scratch_shapes=[
                pltpu.VMEM((rows, 4 * inner), BF16),
                pltpu.VMEM((rows, 128), F32),
                pltpu.VMEM((8, width), F32),
                pltpu.VMEM((block, 4 * inner), BF16),
            ],
        ),
        out_shape=[
            jax.ShapeDtypeStruct((rows, width), F32),
            jax.ShapeDtypeStruct((rows, width), BF16),
        ],
        name="middle_rows",
        compiler_params=params(),
        cost_estimate=cost(5),
    )(where, *pieces, out_all, rows_low, gain)


def load_pieces(where_ref, pieces, weight, sems, base, cols):
    copies = []
    at = 0
    for i in range(len(pieces) if len(pieces) > 1 else 4):
        if len(pieces) > 1:
            piece = pieces[i]
            height = piece.shape[0]
            rows = pl.ds(0, height)
        else:
            piece = pieces[0]
            height = piece.shape[0] // 4
            rows = pl.ds(pl.multiple_of(where_ref[i] * height, 128), height)
        copies.append(
            pltpu.make_async_copy(
                piece.at[rows, cols], weight.at[pl.ds(at, height), :], sems.at[base + i]
            )
        )
        at += height
    return copies


def store(ref, cols, value):
    ref[:, cols] = value.astype(ref.dtype)


def feed_kernel(units, first, last, where_ref, *refs):
    h_own, h_other, c_own, c_other = refs[:4]
    pieces = refs[4 : len(refs) - (4 + (0 if first else 1) + (1 if last else 0))]
    rest = refs[4 + len(pieces) :]
    if not first:
        dh_sum, rest = rest[0], rest[1:]
    act_ref, *dh_refs, weight, sems = rest
    step = pl.program_id(0)

    @pl.when(step == 0)
    def _():
        copies = load_pieces(
            where_ref, pieces, weight, sems, 0, pl.ds(0, weight.shape[1])
        )
        for copy in copies:
            copy.start()
        for copy in copies:
            copy.wait()

    mine = step < 2
    pair = 2 * units
    h = jnp.where(mine, h_own[...], h_other[...])
    c = jnp.where(mine, c_own[...], c_other[...])
    for at in range(0, units, 256):
        cols = slice(at, at + 256)
        gate = mm(h, weight[:, cols])
        up = mm(h, weight[:, units + at : units + at + 256])
        dhidden = mm(c, weight[:, pair + at : pair + at + 256])
        sig = jax.nn.sigmoid(gate)
        silu = gate * sig
        act_ref[:, pair + at : pair + at + 256] = (silu * up).astype(BF16)
        act_ref[:, cols] = (dhidden * up * (sig + silu * (1.0 - sig))).astype(BF16)
        act_ref[:, units + at : units + at + 256] = (dhidden * silu).astype(BF16)
    width = weight.shape[0]
    act = act_ref[:, :pair]
    for at in range(0, width, 512):
        cols = slice(at, at + 512)
        dh = mm_nt(act, weight[cols, :pair])
        if not first:
            dh = dh + dh_sum[:, cols]
        if last:
            pl.when(mine)(functools.partial(store, dh_refs[0], cols, dh))
            pl.when(jnp.logical_not(mine))(functools.partial(store, dh_refs[1], cols, dh))
        else:
            dh_refs[0][:, cols] = dh


def feed_forward_part(where, h2, cot, pieces, total, last):
    rows, width = h2[0].shape
    columns = pieces[0].shape[1]
    tile = rows // 2
    first = total is None
    own = pl.BlockSpec((tile, width), lambda i: (jnp.minimum(i, 1), 0))
    other = pl.BlockSpec((tile, width), lambda i: (jnp.maximum(i - 2, 0), 0))
    flat = pl.BlockSpec((tile, width), lambda i: (i, 0))
    whole = pl.BlockSpec(memory_space=pl.ANY)
    sums = (
        [jax.ShapeDtypeStruct((rows, width), F32), jax.ShapeDtypeStruct((rows, width), BF16)]
        if last
        else [jax.ShapeDtypeStruct((2 * rows, width), F32)]
    )
    return pl.pallas_call(
        functools.partial(feed_kernel, columns // 3, first, last),
        grid=(4,),
        in_specs=[pl.BlockSpec(memory_space=pltpu.SMEM), own, other, own, other]
        + [whole] * len(pieces)
        + ([] if first else [flat]),
        out_specs=[pl.BlockSpec((tile, columns), lambda i: (i, 0))]
        + ([own, other] if last else [flat]),
        out_shape=[jax.ShapeDtypeStruct((2 * rows, columns), BF16)] + sums,
        scratch_shapes=[
            pltpu.VMEM((width, columns), BF16),
            pltpu.SemaphoreType.DMA((max(4, len(pieces)),)),
        ],
        input_output_aliases={} if first or last else {5 + len(pieces): 1},
        name="feed_forward",
        compiler_params=params(),
        cost_estimate=cost(15),
    )(where, *h2, *cot, *pieces, *([] if first else [total]))


def down_kernel(counts, where_ref, *refs):
    chunks = len(counts)
    acts = refs[:chunks]
    pieces = refs[chunks : chunks + sum(counts)]
    own_ref, other_ref, weight, sems = refs[chunks + sum(counts) :]
    units = weight.shape[2]
    step = pl.program_id(0)

    @pl.when(step == 0)
    def _():
        copies = []
        i = 0
        for c, count in enumerate(counts):
            copies += load_pieces(
                where_ref,
                pieces[i : i + count],
                weight.at[c],
                sems,
                len(copies),
                pl.ds(2 * units, units),
            )
            i += count
        for copy in copies:
            copy.start()
        for copy in copies:
            copy.wait()

    for at in range(0, weight.shape[1], 512):
        cols = slice(at, at + 512)
        total = mm_nt(acts[0][...], weight[0, cols, :])
        for c in range(1, chunks):
            total = total + mm_nt(acts[c][...], weight[c, cols, :])
        pl.when(step == 0)(functools.partial(store, own_ref, cols, total))
        pl.when(step == 1)(functools.partial(store, other_ref, cols, total))


def down_rows(where, acts, chunks, width):
    rows = acts[0].shape[0] // 2
    tile = rows
    units = acts[0].shape[1] // 3
    counts = tuple(len(pieces) for pieces in chunks)
    own = pl.BlockSpec((tile, width), lambda i: (0, 0))
    other = own
    return pl.pallas_call(
        functools.partial(down_kernel, counts),
        grid=(2,),
        in_specs=[pl.BlockSpec(memory_space=pltpu.SMEM)]
        + [pl.BlockSpec((tile, units), lambda i: (i, 2))] * len(acts)
        + [pl.BlockSpec(memory_space=pl.ANY)] * sum(counts),
        out_specs=[own, other],
        out_shape=[
            jax.ShapeDtypeStruct((rows, width), F32),
            jax.ShapeDtypeStruct((rows, width), BF16),
        ],
        scratch_shapes=[
            pltpu.VMEM((len(acts), width, units), BF16),
            pltpu.SemaphoreType.DMA((sum(max(4, count) for count in counts),)),
        ],
        name="down_rows",
        compiler_params=params(),
        cost_estimate=cost(10),
    )(where, *acts, *[piece for pieces in chunks for piece in pieces])


def whole_grad_kernel(where_ref, h_ref, c_ref, act, out_ref):
    def work(left):
        value = mm(left[...], act[...]).astype(out_ref.dtype)
        height = value.shape[0] // 2
        for b in range(2):
            at = pl.multiple_of(((where_ref[0] & 1) ^ b) * height, 128)
            out_ref[pl.ds(at, height), :] = value[b * height : (b + 1) * height]

    pl.when(pl.program_id(0) < 2)(functools.partial(work, h_ref))
    pl.when(pl.program_id(0) == 2)(functools.partial(work, c_ref))


def whole_weight_grads(where, h2_t, cot_t, act):
    width, rows = h2_t.shape
    columns = act.shape[1]
    third = columns // 3
    height = width // 2
    return pl.pallas_call(
        whole_grad_kernel,
        grid_spec=pltpu.PrefetchScalarGridSpec(
            num_scalar_prefetch=1,
            grid=(3, 2),
            in_specs=[
                pl.BlockSpec((height, rows), lambda i, j, w: (jnp.where(i < 2, j, 1), 0)),
                pl.BlockSpec((height, rows), lambda i, j, w: (jnp.where(i < 2, 0, j), 0)),
                pl.BlockSpec((rows, third), lambda i, j, w: (0, i)),
            ],
            out_specs=pl.BlockSpec((height, third), lambda i, j, w: ((w[0] >> 1) ^ j, i)),
        ),
        out_shape=jax.ShapeDtypeStruct((width, columns), BF16),
        name="whole_grads",
        compiler_params=params(),
        cost_estimate=cost(10),
    )(where, h2_t, cot_t, act)


def last_grad_kernel(pair, where_ref, h_ref, c_ref, act, *refs):
    added, (own_ref, other_ref, total) = refs[:-3], refs[-3:]
    for cols, left in ((slice(0, pair), h_ref), (slice(pair, None), c_ref)):
        value = mm(left[...], act[:, cols])
        for term in added:
            value = value + term[:, cols].astype(F32)
        total[:, cols] = value
    rows = own_ref.shape[0]
    own_ref[...] = total[pl.ds(pl.multiple_of(where_ref[16] * rows, 64), rows), :]
    other = pl.ds(pl.multiple_of((1 - where_ref[16]) * rows, 64), rows)
    other_ref[...] = total[other, :].astype(BF16)


def last_weight_grads(where, h2_t, cot_t, act, added):
    width, rows = h2_t.shape
    columns = act.shape[1]
    height = width // 4
    left = pl.BlockSpec((height, rows), lambda i: (0, 0))
    tile = pl.BlockSpec((height, columns), lambda i: (0, 0))
    half = pl.BlockSpec((height // 2, columns), lambda i: (0, 0))
    return pl.pallas_call(
        functools.partial(last_grad_kernel, 2 * columns // 3),
        grid=(1,),
        in_specs=[pl.BlockSpec(memory_space=pltpu.SMEM), left, left]
        + [pl.BlockSpec((rows, columns), lambda i: (0, 0))]
        + [tile] * len(added),
        out_specs=[half, half],
        out_shape=[
            jax.ShapeDtypeStruct((height // 2, columns), F32),
            jax.ShapeDtypeStruct((height // 2, columns), BF16),
        ],
        scratch_shapes=[pltpu.VMEM((height, columns), F32)],
        name="last_weight_grad",
        compiler_params=params(),
        cost_estimate=cost(4),
    )(where, h2_t, cot_t, act, *[term for term, _ in added])


def finish_kernel(where_ref, own_ref, recv_ref, *outs):
    half = own_ref.shape[1] // 3
    for i, out in enumerate(outs):
        cols = slice(i * half, (i + 1) * half)
        out[:, column(where_ref[16], half)] = own_ref[:, cols]
        out[:, column(1 - where_ref[16], half)] = recv_ref[:, cols].astype(F32)


def finish_grads(where, own, recv):
    rows, columns = own.shape
    flat = pl.BlockSpec((rows, columns), lambda i: (0, 0))
    wide = pl.BlockSpec((rows, 2 * columns // 3), lambda i: (0, 0))
    return pl.pallas_call(
        finish_kernel,
        grid=(1,),
        in_specs=[pl.BlockSpec(memory_space=pltpu.SMEM), flat, flat],
        out_specs=[wide] * 3,
        out_shape=[jax.ShapeDtypeStruct((rows, 2 * columns // 3), F32)] * 3,
        name="finish_grads",
        compiler_params=params(),
        cost_estimate=cost(2),
    )(where, own, recv)


def grad_kernel(plan, *refs):
    count = len(plan)
    hs, cs, act = refs[:count], refs[count : 2 * count], refs[2 * count]
    extra = list(refs[2 * count + 1 : -1])
    out_ref = refs[-1]
    height = hs[0].shape[0]

    def work(lefts):
        at = 0
        for i, terms in enumerate(plan):
            value = mm(lefts[i][...], act[...])
            for term in extra[at : at + terms]:
                value = value + term[...].astype(F32)
            at += terms
            out_ref[i * height : (i + 1) * height, :] = value.astype(out_ref.dtype)

    pl.when(pl.program_id(0) < 2)(functools.partial(work, hs))
    pl.when(pl.program_id(0) == 2)(functools.partial(work, cs))


def weight_grads(h2_t, cot_t, act, blocks, added):
    width, rows = h2_t.shape
    columns = act.shape[1]
    height = width // 4
    third = columns // 3
    whole = len(blocks) * height
    if blocks == [2, 3]:
        height, blocks, added = 2 * height, [1], [[]]
    left = [pl.BlockSpec((height, rows), lambda i, at=at: (at, 0)) for at in blocks]
    terms = [term for group in added for term in group]
    tiles = [pl.BlockSpec((height, third), lambda i, at=at: (at, i)) for _, at in terms]
    return pl.pallas_call(
        functools.partial(grad_kernel, tuple(len(g) for g in added)),
        grid=(3,),
        in_specs=left + left + [pl.BlockSpec((rows, third), lambda i: (0, i))] + tiles,
        out_specs=pl.BlockSpec((whole, third), lambda i: (0, i)),
        out_shape=jax.ShapeDtypeStruct((whole, columns), BF16),
        name="weight_grads",
        compiler_params=params(),
        cost_estimate=cost(1 + whole // 192),
    )(*([h2_t] * len(blocks)), *([cot_t] * len(blocks)), act, *[term for term, _ in terms])


def norm_two_kernel(
    where_ref, own_ref, recv_ref, mid_ref, cot_ref, gain_ref, w_ref,
    dmid_ref, dm_ref, datt_ref, dgain_ref, weight,
):
    block = gain_ref.shape[1] // 4
    mid = mid_ref[...]
    scale = row_norm(mid)
    gain = jnp.concatenate([gain_ref[:, column(where_ref[j], block)] for j in range(4)], axis=1)
    upstream = own_ref[...] + recv_ref[...].astype(F32)
    weighted = upstream * gain
    inner = jnp.mean(mid * weighted, axis=-1, keepdims=True)
    grad = cot_ref[...].astype(F32) + scale * weighted - mid * (scale * scale * scale) * inner
    dmid_ref[...] = grad
    low = grad.astype(BF16)
    dm_ref[...] = low
    dgain = jnp.sum(upstream * mid * scale, axis=0, keepdims=True)

    @pl.when(pl.program_id(0) == 0)
    def _():
        dgain_ref[...] = jnp.zeros_like(dgain_ref)

    for j in range(4):
        at = column(where_ref[j], block)
        dgain_ref[0:1, at] = dgain_ref[0:1, at] + dgain[:, j * block : (j + 1) * block]
    total = None
    for j in range(4):
        for c in range(2):
            for s in range(4):
                rows, inner_width = w_ref.shape[2:]
                weight[c * rows : (c + 1) * rows, s * inner_width : (s + 1) * inner_width] = w_ref[
                    2 * where_ref[j] + c, s
                ]
        term = mm(low[:, j * block : (j + 1) * block], weight[...])
        total = term if total is None else total + term
    inner_width = datt_ref.shape[3]
    for s in range(4):
        datt_ref[s, 0] = total[:, s * inner_width : (s + 1) * inner_width].astype(BF16)


def norm_two(where, own, recv, middle, cot, gain, out_all, count):
    rows, width = middle.shape
    part = rows // count
    inner = out_all.shape[3]
    flat = pl.BlockSpec((part, width), lambda i, w: (i, 0))
    row = pl.BlockSpec((1, width), lambda i, w: (0, 0))
    return pl.pallas_call(
        norm_two_kernel,
        grid_spec=pltpu.PrefetchScalarGridSpec(
            num_scalar_prefetch=1,
            grid=(count,),
            in_specs=[flat] * 4
            + [row, pl.BlockSpec(out_all.shape, lambda i, w: (0, 0, 0, 0))],
            out_specs=[
                flat,
                flat,
                pl.BlockSpec((4, 1, part, inner), lambda i, w: (0, i, 0, 0)),
                row,
            ],
            scratch_shapes=[pltpu.VMEM((width // 4, 4 * inner), BF16)],
        ),
        out_shape=[
            jax.ShapeDtypeStruct((rows, width), F32),
            jax.ShapeDtypeStruct((rows, width), BF16),
            jax.ShapeDtypeStruct((4, count, part, inner), BF16),
            jax.ShapeDtypeStruct((1, width), F32),
        ],
        name="norm_two",
        compiler_params=params(),
        cost_estimate=cost(6),
    )(where, own, recv, middle, cot, gain, out_all)


def dh1_kernel(where_ref, d_ref, l_ref, h_ref, w_ref, small_ref, gain_ref, out_ref, dgain_ref):
    columns = d_ref.shape[1]
    step = pl.program_id(0)

    @pl.when(step == 0)
    def _():
        dgain_ref[...] = jnp.zeros_like(dgain_ref)

    grads = d_ref[...]
    for at in range(0, w_ref.shape[0], 512):
        cols = slice(at, at + 512)
        total = mm_nt(grads, w_ref[cols, :columns]) + mm_tn(l_ref[...], small_ref[:, cols])
        out_ref[0, :, cols] = total.astype(BF16)
        part = jnp.sum(total * h_ref[:, cols].astype(F32), axis=0, keepdims=True)
        dgain_ref[:, cols] = dgain_ref[:, cols] + part

    @pl.when(step == 3)
    def _():
        dgain_ref[...] = dgain_ref[...] / gain_ref[...]


def dh1_pieces(where, dprojected, dlogits, normed, weight, small, gain):
    rows, columns = dprojected.shape
    width = weight.shape[0]
    part = rows // 4
    whole = lambda shape: pl.BlockSpec(shape, lambda i, w: (0, 0))
    return pl.pallas_call(
        dh1_kernel,
        grid_spec=pltpu.PrefetchScalarGridSpec(
            num_scalar_prefetch=1,
            grid=(4,),
            in_specs=[
                pl.BlockSpec((part, columns), lambda i, w: (w[7 - i], 0)),
                pl.BlockSpec((dlogits.shape[0], part), lambda i, w: (0, w[7 - i])),
                pl.BlockSpec((part, width), lambda i, w: (w[7 - i], 0)),
                whole(weight.shape),
                whole(small.shape),
                whole(gain.shape),
            ],
            out_specs=[
                pl.BlockSpec((1, part, width), lambda i, w: (3 - i, 0, 0)),
                whole(gain.shape),
            ],
        ),
        out_shape=[
            jax.ShapeDtypeStruct((4, part, width), BF16),
            jax.ShapeDtypeStruct(gain.shape, F32),
        ],
        name="dh1_rows",
        compiler_params=params(),
        cost_estimate=cost(0.008),
    )(where, dprojected, dlogits, normed, weight, small, gain)


def store_cores(where_ref, out_ref, cols, values):
    rows = values.shape[0] // 2
    for c in range(2):
        out_ref[jnp.where(where_ref[16] == c, 0, 1), :, cols] = values[
            c * rows : (c + 1) * rows
        ]


def attn_grad_kernel(count, beta, where_ref, *refs):
    hs, ds, ls = refs[:count], refs[count : 2 * count], refs[2 * count : 3 * count]
    gains, gain_two, out_ref = refs[3 * count : 4 * count], refs[4 * count], refs[4 * count + 1]
    columns = ds[0].shape[1]
    lefts = [h[...].T for h in hs]
    for at in range(0, columns, 512):
        cols = slice(at, at + 512)
        total = mm(lefts[0], ds[0][:, cols])
        for i in range(1, count):
            total = total + mm(lefts[i], ds[i][:, cols])
        store_cores(where_ref, out_ref, cols, total.astype(BF16))
    small = mm_nt(lefts[0], ls[0][...])
    for i in range(1, count):
        small = small + mm_nt(lefts[i], ls[i][...])
    gain_one = gains[0][...]
    for i in range(1, count):
        gain_one = gain_one + gains[i][...]
    extra = ls[0].shape[0]
    width = gain_one.shape[1]
    line = lax.broadcasted_iota(jnp.int32, (extra, width), 0)
    rows = jnp.where(line == beta, gain_one, jnp.where(line == beta + 1, gain_two[...], 0.0))
    eye = lax.broadcasted_iota(jnp.int32, (extra, extra), 0) == lax.broadcasted_iota(
        jnp.int32, (extra, extra), 1
    )
    small = small + mm_tn(rows, eye.astype(BF16))
    store_cores(where_ref, out_ref, slice(columns, None), small.astype(BF16))


def attn_grads(where, normed, dprojected, dlogits, gains, gain_two, beta):
    rows, width = normed[0].shape
    columns = dprojected[0].shape[1]
    extra = dlogits[0].shape[0]
    count = len(normed)
    block = width // 4
    whole = lambda shape: pl.BlockSpec(shape, lambda i: (0, 0))
    return pl.pallas_call(
        functools.partial(attn_grad_kernel, count, beta),
        grid=(4,),
        in_specs=[pl.BlockSpec(memory_space=pltpu.SMEM)]
        + [pl.BlockSpec((rows, block), lambda i: (0, i))] * count
        + [whole((rows, columns))] * count
        + [whole((extra, rows))] * count
        + [pl.BlockSpec((1, block), lambda i: (0, i))] * (count + 1),
        out_specs=pl.BlockSpec((2, block // 2, columns + extra), lambda i: (0, i, 0)),
        out_shape=jax.ShapeDtypeStruct((2, width // 2, columns + extra), BF16),
        name="attn_grads",
        compiler_params=params(),
        cost_estimate=cost(14),
    )(where, *normed, *dprojected, *dlogits, *gains, gain_two)


def out_grad_kernel(pieces, where_ref, *refs):
    dm_ref, out_ref, att = refs[pieces:]

    @pl.when(pl.program_id(0) == 0)
    def _():
        gather_pieces(refs[:pieces], att, 4)

    total = mm_tn(dm_ref[...], att[...]).astype(BF16)
    rows, inner = out_ref.shape[3:]
    for c in range(2):
        for s in range(4):
            out_ref[jnp.where(where_ref[16] == c, 0, 1), 0, s] = total[
                c * rows : (c + 1) * rows, s * inner : (s + 1) * inner
            ]


def out_grads(where, pieces, dm):
    rows, width = dm.shape
    part, inner = pieces[0].shape
    block = width // 4
    return pl.pallas_call(
        functools.partial(out_grad_kernel, len(pieces)),
        grid_spec=pltpu.PrefetchScalarGridSpec(
            num_scalar_prefetch=1,
            grid=(4,),
            in_specs=[pl.BlockSpec((part, inner), lambda i, w: (0, 0))] * len(pieces)
            + [pl.BlockSpec((rows, block), lambda i, w: (0, i))],
            out_specs=pl.BlockSpec((2, 1, 4, block // 2, inner), lambda i, w: (0, w[i], 0, 0, 0)),
            scratch_shapes=[pltpu.VMEM((rows, 4 * inner), BF16)],
        ),
        out_shape=jax.ShapeDtypeStruct((2, 4, 4, block // 2, inner), BF16),
        name="out_grads",
        compiler_params=params(),
        cost_estimate=cost(5),
    )(where, *pieces, dm)


def block_out_kernel(where_ref, mid_ref, own_ref, recv_ref, out_ref):
    total = mid_ref[...] + own_ref[...] + recv_ref[...].astype(F32)
    out_ref[...] = total.astype(out_ref.dtype)


def block_out_rows(where, middle, own, recv):
    rows, width = middle.shape
    block = width // 4
    flat = pl.BlockSpec((rows, block), lambda i, w: (0, i))
    return pl.pallas_call(
        block_out_kernel,
        grid_spec=pltpu.PrefetchScalarGridSpec(
            num_scalar_prefetch=1,
            grid=(4,),
            in_specs=[flat] * 3,
            out_specs=pl.BlockSpec((rows, block), lambda i, w: (0, w[i])),
        ),
        out_shape=jax.ShapeDtypeStruct((rows, width), BF16),
        name="block_out",
        compiler_params=params(),
        cost_estimate=cost(4),
    )(where, middle, own, recv)


def input_grad_kernel(where_ref, x_ref, own_ref, recv_ref, dmid_ref, gain_ref, *refs):
    out_ref = refs[-1]
    rows = x_ref[...].astype(F32)
    scale = row_norm(rows)
    weighted = (own_ref[...].astype(F32) + recv_ref[...].astype(F32)) * gain_ref[...]
    inner = jnp.mean(rows * weighted, axis=-1, keepdims=True)
    out_ref[...] = scale * weighted - rows * (scale * scale * scale) * inner
    block = rows.shape[1] // 4
    for j in range(4):
        at = column(where_ref[j], block)
        out_ref[:, at] = out_ref[:, at] + dmid_ref[:, j * block : (j + 1) * block]


def input_grad_rows(where, rows_low, pieces, recv, dmiddle, gain, batch, total):
    _, part, width = pieces.shape
    own = pl.BlockSpec((None, part // 2, width), lambda i, w: (0, i, 0))
    flat = pl.BlockSpec((part // 2, width), lambda i, w: (i, 0))
    later = pl.BlockSpec((part // 2, width), lambda i, w: (i + 2 * batch, 0))
    first = total is None
    return pl.pallas_call(
        input_grad_kernel,
        grid_spec=pltpu.PrefetchScalarGridSpec(
            num_scalar_prefetch=1,
            grid=(2,),
            in_specs=[later, own, flat, later, pl.BlockSpec((1, width), lambda i, w: (0, 0))]
            + ([] if first else [pl.BlockSpec(memory_space=pl.ANY)]),
            out_specs=later,
        ),
        out_shape=jax.ShapeDtypeStruct(dmiddle.shape, F32),
        input_output_aliases={} if first else {6: 0},
        name="input_grad",
        compiler_params=params(),
        cost_estimate=cost(3),
    )(where, rows_low, pieces, recv, dmiddle, gain, *([] if first else [total]))


def product(left_side, right_side):
    return jnp.dot(left_side, right_side, preferred_element_type=F32)


def by_transposed(left_side, right_side):
    return lax.dot_general(
        left_side, right_side, (((1,), (1,)), ((), ())), preferred_element_type=F32
    )


def transposed_by(left_side, right_side):
    return lax.dot_general(
        left_side, right_side, (((0,), (0,)), ((), ())), preferred_element_type=F32
    )


def shift(values, axis, step):
    size = lax.axis_size(axis)
    return lax.ppermute(values, axis, [(i, (i + step) % size) for i in range(size)])


def ring_gather(values, axis):
    pieces = [values]
    for _ in range(lax.axis_size(axis) - 1):
        pieces.append(shift(pieces[-1], axis, 1))
    return pieces


def ring_scatter(pieces, axis):
    total = pieces[-1].astype(BF16)
    for piece in pieces[-2::-1]:
        total = shift(total, axis, -1).astype(F32) + piece.astype(F32)
        if piece is not pieces[0]:
            total = total.astype(BF16)
    return total


def row_scale(rows):
    return lax.rsqrt(jnp.mean(rows * rows, axis=-1, keepdims=True) + 1e-06)


def norm_back(rows, scale, gain, upstream):
    weighted = upstream * gain
    inner = jnp.mean(rows * weighted, axis=-1, keepdims=True)
    grad = scale * weighted - rows * (scale * scale * scale) * inner
    return grad, jnp.sum(upstream * rows * scale, axis=0)


def place(pieces, axis, order):
    size = lax.axis_size(axis)
    index = lax.axis_index(axis)
    height = pieces[0].shape[0]
    whole = jnp.zeros((size * height,) + pieces[0].shape[1:], pieces[0].dtype)
    for s, piece in enumerate(pieces):
        at = ((index + order * s) % size) * height
        whole = lax.dynamic_update_slice_in_dim(whole, piece, at, 0)
    return whole


def cut(whole, axis, step):
    size = lax.axis_size(axis)
    height = whole.shape[0] // size
    at = ((lax.axis_index(axis) + step) % size) * height
    return lax.dynamic_slice_in_dim(whole, at, height, 0)


def by_core(own, other, axis):
    first = lax.axis_index("core") == 0
    return jnp.where(
        first, jnp.concatenate([own, other], axis), jnp.concatenate([other, own], axis)
    )


def general_body(
    tokens,
    lengths,
    cotangent,
    q_weight,
    k_weight,
    v_weight,
    direction_weight,
    beta_weight,
    out_weight,
    gate_weight,
    up_weight,
    down_weight,
    norm_gain_one,
    norm_gain_two,
):
    zsize = lax.axis_size("head")
    core = lax.axis_index("core")
    plane = ("da", "db")
    dp = ("da", "db", "core")
    micro, slots, part, width = tokens.shape
    count = micro * slots
    local = count * part
    shard = q_weight.shape[0]
    heads = beta_weight.shape[1]
    inner = heads * HEAD_DIM
    half = gate_weight.shape[1] // 2
    rows_low = tokens.reshape(count, part, width)
    rows_in = rows_low.reshape(local, width).astype(F32)
    cot_own = cotangent.reshape(local, width)
    seq_lengths = lengths.reshape(count)

    sequences = [place(ring_gather(rows_low[i], "head"), "head", -1) for i in range(count)]

    small = jnp.concatenate(
        [beta_weight.T, norm_gain_one[None, :], norm_gain_two[None, :]], axis=0
    )
    small = lax.all_gather(small, dp, axis=1, tiled=True)
    beta_rows = small[:heads]
    gain_one = small[heads].astype(F32)
    gain_two = small[heads + 1].astype(F32)
    attn_local = jnp.stack(
        [w.reshape(shard, heads, HEAD_DIM) for w in (q_weight, k_weight, v_weight, direction_weight)],
        axis=2,
    ).reshape(shard, 4 * inner)
    attn_weight = lax.all_gather(attn_local, dp, axis=0, tiled=True)
    out_pieces = ring_gather(out_weight.T, "head")
    out_all = jnp.concatenate(out_pieces, axis=1)
    out_all = lax.all_gather(out_all, dp, axis=0, tiled=True)
    ffn_local = jnp.concatenate(
        [w.reshape(shard, 2, half) for w in (gate_weight, up_weight, down_weight.T)], axis=2
    )
    ffn_own = lax.dynamic_index_in_dim(ffn_local, core, 1, keepdims=False)
    ffn_other = lax.dynamic_index_in_dim(ffn_local, 1 - core, 1, keepdims=False)
    ffn_other = shift(ffn_other, "core", 1)
    ffn_chip = by_core(ffn_own, ffn_other, 0)
    ffn_weight = [
        lax.all_gather(w, plane, axis=0, tiled=True) for w in ring_gather(ffn_chip, "head")
    ]

    normed, projected, logits, kept, mixed = [], [], [], [], []
    for i in range(count):
        rows = sequences[i].astype(F32)
        h1 = (rows * row_scale(rows) * gain_one).astype(BF16)
        normed.append(h1)
        projected.append(product(h1, attn_weight).astype(BF16))
        logits.append(by_transposed(beta_rows, h1))
        result = attention_forward(None, seq_lengths[i : i + 1], projected[i], logits[i])
        kept.append(result[1:])
        pieces = [cut(result[0], "head", 0)]
        for s in range(1, zsize):
            pieces.append(shift(cut(result[0], "head", s), "head", s))
        mixed.append(jnp.concatenate(pieces, axis=1))
    attended = jnp.concatenate(mixed, axis=0)
    middle = rows_in + by_transposed(attended, out_all)
    scale_two = row_scale(middle)
    h2_own = (middle * scale_two * gain_two).astype(BF16)
    h2 = jnp.concatenate([h2_own, shift(h2_own, "core", 1)], axis=0)
    cot = jnp.concatenate([cot_own, shift(cot_own, "core", 1)], axis=0)

    out_sum = None
    dh2_sum = None
    ffn_terms = []
    for weight in ffn_weight:
        gate_up = product(h2, weight[:, : 2 * half])
        dhidden = product(cot, weight[:, 2 * half :])
        gate = gate_up[:, :half]
        up = gate_up[:, half:]
        sig = jax.nn.sigmoid(gate)
        hidden = (gate * sig * up).astype(BF16)
        dgate = (dhidden * up * sig * (1.0 + gate * (1.0 - sig))).astype(BF16)
        dup = (dhidden * gate * sig).astype(BF16)
        dgate_up = jnp.concatenate([dgate, dup], axis=1)
        out_part = by_transposed(hidden, weight[:, 2 * half :])
        dh2_part = by_transposed(dgate_up, weight[:, : 2 * half])
        out_sum = out_part if out_sum is None else out_sum + out_part
        dh2_sum = dh2_part if dh2_sum is None else dh2_sum + dh2_part
        ffn_terms.append(
            jnp.concatenate(
                [
                    transposed_by(h2, dgate_up).astype(BF16),
                    transposed_by(cot, hidden).astype(BF16),
                ],
                axis=1,
            )
        )
    dh2 = dh2_sum[:local] + shift(dh2_sum[local:].astype(BF16), "core", 1).astype(F32)
    down = out_sum[:local] + shift(out_sum[local:].astype(BF16), "core", 1).astype(F32)
    block_out = (middle + down).astype(BF16)
    dmid, gain_two_grad = norm_back(middle, scale_two, gain_two, dh2)
    dmiddle = cot_own.astype(F32) + dmid
    dm = dmiddle.astype(BF16)
    dattended = product(dm, out_all).astype(BF16)
    out_term = transposed_by(dm, attended).astype(BF16)

    attn_term = None
    beta_term = None
    dh1_parts = []
    for i in range(count):
        rows = dattended[i * part : (i + 1) * part]
        pieces = [rows[:, :inner]]
        for s in range(1, zsize):
            pieces.append(shift(rows[:, s * inner : (s + 1) * inner], "head", -s))
        grad_out = place(pieces, "head", 1)
        dprojected, dlogits = attention_backward(
            None, seq_lengths[i : i + 1], projected[i], logits[i], [grad_out[None]], 0, kept[i]
        )
        dlogits = dlogits.astype(BF16)
        dh1 = by_transposed(dprojected, attn_weight) + transposed_by(dlogits, beta_rows)
        dh1 = dh1.astype(BF16)
        dh1_parts.append(ring_scatter([cut(dh1, "head", -s) for s in range(zsize)], "head"))
        term = transposed_by(normed[i], dprojected)
        attn_term = term if attn_term is None else attn_term + term
        term = product(dlogits, normed[i])
        beta_term = term if beta_term is None else beta_term + term
    dh1 = jnp.concatenate(dh1_parts, axis=0)
    scale_one = row_scale(rows_in)
    drows, gain_one_grad = norm_back(rows_in, scale_one, gain_one, dh1)
    input_grad = dmiddle + drows

    ffn_total = ring_scatter(
        [lax.psum_scatter(t, plane, scatter_dimension=0, tiled=True) for t in ffn_terms], "head"
    )
    ffn_total = ffn_total.reshape(2, shard, 3 * half)
    own = lax.dynamic_index_in_dim(ffn_total, core, 0, keepdims=False)
    other = lax.dynamic_index_in_dim(ffn_total, 1 - core, 0, keepdims=False)
    other = shift(other.astype(BF16), "core", 1).astype(F32)
    gate_grad, up_grad, down_grad = [
        by_core(own[:, j * half : (j + 1) * half], other[:, j * half : (j + 1) * half], 1)
        for j in range(3)
    ]
    out_total = lax.psum_scatter(out_term, dp, scatter_dimension=0, tiled=True)
    out_total = ring_scatter(
        [out_total[:, s * inner : (s + 1) * inner] for s in range(zsize)], "head"
    )
    attn_total = lax.psum_scatter(attn_term.astype(BF16), dp, scatter_dimension=0, tiled=True)
    attn_total = attn_total.astype(F32).reshape(shard, heads, 4, HEAD_DIM)
    small_term = jnp.concatenate(
        [beta_term, gain_one_grad[None, :], gain_two_grad[None, :]], axis=0
    )
    small_total = lax.psum_scatter(small_term, dp, scatter_dimension=1, tiled=True)
    gain_grads = lax.psum(small_total[heads:], "head")
    shape = (micro, slots, part, width)
    return (
        block_out.reshape(shape),
        input_grad.reshape(shape),
        attn_total[:, :, 0].reshape(shard, inner),
        attn_total[:, :, 1].reshape(shard, inner),
        attn_total[:, :, 2].reshape(shard, inner),
        attn_total[:, :, 3].reshape(shard, inner),
        small_total[:heads].T,
        out_total.T,
        gate_grad,
        up_grad,
        down_grad.T,
        gain_grads[0],
        gain_grads[1],
    )


def after(values, others):
    return lax.optimization_barrier((values, others))[0]


def swap(values, axis, mask):
    size = lax.axis_size(axis)
    return lax.ppermute(values, axis, [(i, i ^ mask) for i in range(size)])


def plane_swap(values, mask):
    return lax.ppermute(values, ("da", "db"), [(i, i ^ mask) for i in range(4)])


class Plan:
    def __init__(self):
        self.made = {}
        self.waiting = []
        self.last = None

    def get(self, name):
        return self.made[name]

    def send(self, name, needs, start):
        self.waiting.append((name, needs, start))
        self.flush()

    def flush(self):
        progress = True
        while progress:
            progress = False
            for item in list(self.waiting):
                name, needs, start = item
                gates = PLAN["gates"].get(name, [])
                if all(need in self.made for need in list(needs) + list(gates)):
                    self.waiting.remove(item)
                    values = [self.made[need] for need in needs]
                    if gates:
                        values[0] = after(values[0], [self.made[gate] for gate in gates])
                    self.made[name] = start(*values)
                    progress = True

    def put(self, name, value):
        self.made[name] = value
        self.flush()

    def step(self, name, value, work):
        holds = [self.made[pin] for pin in PLAN["pins"].get(name, []) if pin in self.made]
        if self.last is not None:
            holds.append(self.last)
        result = work(after(value, holds) if holds else value)
        self.last = result[0] if isinstance(result, (tuple, list)) else result
        self.put(name, result)


def body(
    tokens,
    lengths,
    cotangent,
    q_weight,
    k_weight,
    v_weight,
    direction_weight,
    beta_weight,
    out_weight,
    gate_weight,
    up_weight,
    down_weight,
    norm_gain_one,
    norm_gain_two,
):
    plan = Plan()
    get, put, send, step = plan.get, plan.put, plan.send, plan.step
    core = lax.axis_index("core")
    z = lax.axis_index("head")
    plane_at = [
        (lax.axis_index("da") ^ a) * 2 + (lax.axis_index("db") ^ b)
        for a in range(2)
        for b in range(2)
    ]
    where = jnp.stack(
        plane_at
        + [(z - s) % 4 for s in range(4)]
        + [(z + s) % 4 for s in range(4)]
        + [(p - z) % 4 for p in range(4)]
        + [core]
    ).astype(jnp.int32)
    dp = ("da", "db", "core")
    micro, slots, part, width = tokens.shape
    count = micro * slots
    local = count * part
    shard = q_weight.shape[0]
    heads = beta_weight.shape[1]
    inner = heads * HEAD_DIM
    columns = 4 * inner
    half = gate_weight.shape[1] // 2
    rows_low = tokens.reshape(count, part, width)
    flat_low = rows_low.reshape(local, width)
    cot_own = cotangent.reshape(local, width)
    seq_lengths = lengths.reshape(count)
    ahead = lambda values: shift(values, "head", 1)
    back = lambda values: shift(values, "head", -1)

    attn_local = jnp.stack(
        [w.reshape(shard, heads, HEAD_DIM) for w in (q_weight, k_weight, v_weight, direction_weight)],
        axis=2,
    ).reshape(shard, columns)
    small = jnp.concatenate(
        [beta_weight, norm_gain_one[:, None], norm_gain_two[:, None]], axis=1
    )
    small = jnp.pad(small, ((0, 0), (0, 128 - small.shape[1])))
    put(ATTN_ROWS, jnp.concatenate([attn_local, small], axis=1))
    put(OUT_ROWS, out_weight.T)
    ffn_local = jnp.concatenate(
        [w.reshape(shard, 2, half) for w in (gate_weight, up_weight, down_weight.T)], axis=2
    )
    put(FFN_OWN, lax.dynamic_index_in_dim(ffn_local, core, 1, keepdims=False))
    put(FFN_GIVE, lax.dynamic_index_in_dim(ffn_local, 1 - core, 1, keepdims=False))
    put(COT, cot_own)

    send(ATTN, [ATTN_ROWS], lambda v: lax.all_gather(v, dp, axis=0, tiled=True))
    send(FFN_TAKE, [FFN_GIVE], lambda v: swap(v, "core", 1))
    send((HOP, 0), [FFN_TAKE, FFN_OWN], lambda take, own: by_core(own, take, 0))
    for i in range(count):
        put((TOK, i, 0), rows_low[i])
        for s in range(1, 4):
            send((TOK, i, s), [(TOK, i, s - 1)], ahead)
    for s in range(1, 4):
        send((HOP, s), [(HOP, s - 1)], ahead)
    for s in range(4):
        if s in PLAN["direct"]:
            for mask in range(1, 4):
                send((CHUNK, s, mask), [(HOP, s)], lambda v, mask=mask: plane_swap(v, mask))
        else:
            send(
                (CHUNK, s, 0),
                [(HOP, s)],
                lambda v: lax.all_gather(v, ("da", "db"), axis=0, tiled=True),
            )
    for s in range(1, 4):
        send((OUT, s), [OUT_ROWS], lambda v, s=s: shift(v, "head", s))
    send(
        OUT_ALL,
        [(OUT, 1), (OUT, 2), (OUT, 3)],
        lambda *v: lax.all_gather(
            jnp.concatenate([out_weight.T] + list(v), axis=0), dp, axis=0, tiled=True
        ),
    )
    send(COT_OTHER, [COT], lambda v: swap(v, "core", 1))

    def chunk(s):
        if s in PLAN["direct"]:
            return [get((HOP, s))] + [get((CHUNK, s, mask)) for mask in range(1, 4)]
        return [get((CHUNK, s, 0))]

    def small_rows():
        turned_small = get(ATTN)[:, columns:].T
        gains = [turned_small[heads + i : heads + i + 1].astype(F32) for i in range(2)]
        return turned_small[:8], gains[0], gains[1]

    def mixed():
        pieces = []
        for i in range(count):
            pieces += [get((ATTEND, i))[0][0]] + [get((MIX, i, s)) for s in range(1, 4)]
        return pieces

    def project_step(i):
        small8, gain_one, _ = small_rows()
        pieces = [get((TOK, i, s)) for s in range(1, 4)]
        step(
            (PROJECT, i),
            rows_low[i],
            lambda v: project(where, [v] + pieces, get(ATTN), small8, gain_one, columns)[::-1],
        )

    def forward_step(i):
        logit, packed, _ = get((PROJECT, i))
        step(
            (ATTEND, i),
            packed,
            lambda v: attention_forward(where, seq_lengths[i : i + 1], v, logit),
        )
        for s in range(1, 4):
            send((MIX, i, s), [(ATTEND, i)], lambda v, s=s: shift(v[0][s], "head", s))

    def turn_cot():
        step(
            TURN_COT, cot_own, lambda v: turned(where, v, get(COT_OTHER), True)
        )

    def middle_step():
        pieces = mixed()
        out_all = get(OUT_ALL).reshape(8, 4, shard, inner)
        _, _, gain_two = small_rows()
        step(
            MIDDLE,
            pieces[0],
            lambda v: middle_rows(where, [v] + pieces[1:], out_all, flat_low, gain_two)[::-1],
        )
        send(H2_OTHER, [MIDDLE], lambda v: swap(v[0], "core", 1))

    def feed_step(s):
        total = get((FEED, s - 1))[1] if s else None
        h2 = get(MIDDLE)[0]
        step(
            (FEED, s),
            h2,
            lambda v: feed_forward_part(
                where, (v, get(H2_OTHER)), get(TURN_COT)[:2], chunk(s), total, s == 3
            ),
        )
        if s == 3:
            send(DH_OTHER, [(FEED, 3)], lambda v: swap(v[2], "core", 1))

    def turn_h2():
        step(TURN_H2, get(MIDDLE)[0], lambda v: turned(where, v, get(H2_OTHER), False)[0])

    def grads(name, c, blocks, added):
        step(
            name,
            get((FEED, c))[0],
            lambda v: weight_grads(get(TURN_H2), get(TURN_COT)[2], v, blocks, added),
        )

    def far_step(c):
        if c in PLAN["whole"]:
            step(
                (GRAD_FAR, c),
                get((FEED, c))[0],
                lambda v: whole_weight_grads(where, get(TURN_H2), get(TURN_COT)[2], v),
            )
            send(
                (PLANE_SUM, c),
                [(GRAD_FAR, c)],
                lambda v: lax.psum_scatter(v, ("da", "db"), scatter_dimension=0, tiled=True),
            )
            if c == 1:
                send((SUM, c), [(PLANE_SUM, c)], ahead)
            else:
                send(
                    (SUM, c),
                    [(PLANE_SUM, c), (SUM, c - 1)],
                    lambda v, last: ahead((v.astype(F32) + last.astype(F32)).astype(BF16)),
                )
            return
        first = c in PLAN["da_first"]
        grads((GRAD_FAR, c), c, [2, 3] if first else [1, 3], [[], []])
        send((FAR, c), [(GRAD_FAR, c)], lambda v: swap(v, "da" if first else "db", 1))

    def middle_grads(c):
        if c in PLAN["whole"]:
            return
        first = c in PLAN["da_first"]
        grads((GRAD_MIDDLE, c), c, [1] if first else [2], [[(get((FAR, c)), 1)]])
        send((MID, c), [(GRAD_MIDDLE, c)], lambda v: swap(v, "db" if first else "da", 1))

    def near_terms(c):
        terms = [(get((FAR, c)), 0), (get((MID, c)), 0)]
        return terms + ([(get((SUM, (c - 1) % 4)), 0)] if c != 1 else [])

    def near_step(c):
        if c in PLAN["whole"]:
            return
        grads((GRAD_NEAR, c), c, [0], [near_terms(c)])
        send((SUM, c), [(GRAD_NEAR, c)], ahead)

    def last_step():
        step(
            LAST,
            get((FEED, 0))[0],
            lambda v: last_weight_grads(where, get(TURN_H2), get(TURN_COT)[2], v, near_terms(0)),
        )
        send(LAST_OTHER, [LAST], lambda v: swap(v[1], "core", 1))

    def norm_step():
        _, _, gain_two = small_rows()
        out_all = get(OUT_ALL).reshape(8, 4, shard, inner)
        step(
            NORM,
            get((FEED, 3))[1],
            lambda v: norm_two(
                where, v, get(DH_OTHER), get(MIDDLE)[1], get(TURN_COT)[0], gain_two, out_all, count
            ),
        )
        for s in range(1, 4):
            send((SENT, s), [NORM], lambda v, s=s: shift(v[2][s], "head", -s))

    def out_step():
        step(OUT_GRAD, get(NORM)[1], lambda v: out_grads(where, mixed(), v))
        send(OUT_CORE, [OUT_GRAD], lambda v: swap(v[1], "core", 1))
        send(
            OUT_RS,
            [OUT_GRAD, OUT_CORE],
            lambda v, other: lax.psum_scatter(
                (v[0].astype(F32) + other.astype(F32)).astype(BF16).reshape(16 * shard, inner),
                ("da", "db"),
                scatter_dimension=0,
                tiled=True,
            ),
        )
        for s in range(1, 4):
            send(
                (OUTSUM, s),
                [OUT_RS, (OUTSUM, s - 1)] if s > 1 else [OUT_RS],
                lambda v, *last, s=s: back(
                    (last[0].astype(F32) + v[(4 - s) * shard : (5 - s) * shard].astype(F32)).astype(
                        BF16
                    )
                    if last
                    else v[3 * shard :]
                ),
            )

    def down_step():
        chunks = [chunk(s) for s in range(4)]
        step(
            DOWN,
            get((FEED, 0))[0],
            lambda v: down_rows(
                where, [v] + [get((FEED, s))[0] for s in range(1, 4)], chunks, width
            ),
        )
        send(DOWN_OTHER, [DOWN], lambda v: swap(v[1], "core", 1))

    def backward_step(i):
        logit, packed, _ = get((PROJECT, i))
        sent = [get(NORM)[2][0]] + [get((SENT, s)) for s in range(1, 4)]
        step(
            (BACK, i),
            packed,
            lambda v: attention_backward(
                where, seq_lengths[i : i + 1], v, logit, sent, i, get((ATTEND, i))[1:]
            ),
        )

    def dh1_step(i):
        small8, gain_one, _ = small_rows()
        dpacked, dlogit = get((BACK, i))
        normed = get((PROJECT, i))[2]
        step(
            (DH, i),
            dpacked,
            lambda v: dh1_pieces(where, v, dlogit, normed, get(ATTN), small8, gain_one),
        )
        send((RING, i, 1), [(DH, i)], lambda v: back(v[0][3]))
        for s in (2, 3):
            send(
                (RING, i, s),
                [(RING, i, s - 1), (DH, i)],
                lambda v, d, s=s: back(
                    (v.astype(F32) + d[0][4 - s].astype(F32)).astype(BF16)
                ),
            )

    def attn_step():
        step(
            ATTN_GRAD,
            get((BACK, 0))[0],
            lambda v: attn_grads(
                where,
                [get((PROJECT, i))[2] for i in range(count)],
                [v] + [get((BACK, i))[0] for i in range(1, count)],
                [get((BACK, i))[1] for i in range(count)],
                [get((DH, i))[1] for i in range(count)],
                get(NORM)[3],
                heads,
            ),
        )
        send(ATTN_CORE, [ATTN_GRAD], lambda v: swap(v[1], "core", 1))
        send(
            ATTN_RS,
            [ATTN_GRAD, ATTN_CORE],
            lambda v, other: lax.psum_scatter(
                (v[0].astype(F32) + other.astype(F32)).astype(BF16),
                ("da", "db"),
                scatter_dimension=0,
                tiled=True,
            ).astype(F32),
        )
        send((GAIN, 0), [ATTN_RS], lambda v: v[:, columns + heads : columns + heads + 2].T)
        send((GAIN, 1), [(GAIN, 0)], lambda v: v + swap(v, "head", 1))
        send((GAIN, 2), [(GAIN, 1)], lambda v: v + swap(v, "head", 2))

    def input_step(i):
        _, gain_one, _ = small_rows()
        total = get((INPUT, 0)) if i else None
        step(
            (INPUT, i),
            get(NORM)[0],
            lambda v: input_grad_rows(
                where, flat_low, get((DH, i))[0], get((RING, i, 3)), v, gain_one, i, total
            ),
        )

    def block_step():
        step(
            BLOCK_OUT,
            get(MIDDLE)[1],
            lambda v: block_out_rows(where, v, get(DOWN)[0], get(DOWN_OTHER)),
        )

    def finish_step():
        step(FINISH, get(LAST)[0], lambda v: finish_grads(where, v, get(LAST_OTHER)))

    steps = {TURN_COT: turn_cot, MIDDLE: middle_step, TURN_H2: turn_h2, NORM: norm_step, OUT_GRAD: out_step}
    steps |= {DOWN: down_step, ATTN_GRAD: attn_step, BLOCK_OUT: block_step, LAST: last_step}
    steps[FINISH] = finish_step
    for i in range(2):
        steps[(PROJECT, i)] = functools.partial(project_step, i)
        steps[(ATTEND, i)] = functools.partial(forward_step, i)
        steps[(BACK, i)] = functools.partial(backward_step, i)
        steps[(DH, i)] = functools.partial(dh1_step, i)
        steps[(INPUT, i)] = functools.partial(input_step, i)
    for c in range(4):
        steps[(FEED, c)] = functools.partial(feed_step, c)
        steps[(GRAD_FAR, c)] = functools.partial(far_step, c)
        steps[(GRAD_MIDDLE, c)] = functools.partial(middle_grads, c)
        if c:
            steps[(GRAD_NEAR, c)] = functools.partial(near_step, c)
    for name in PLAN["order"]:
        steps[name]()

    attn_total = get(ATTN_RS)
    beta_grad = attn_total[:, columns : columns + heads]
    attn_total = attn_total[:, :columns].reshape(shard, heads, 4, HEAD_DIM)
    gate_grad, up_grad, down_grad = get(FINISH)
    gains = get((GAIN, 2))
    shape = (micro, slots, part, width)
    return (
        get(BLOCK_OUT).reshape(shape),
        get((INPUT, 1)).reshape(shape),
        attn_total[:, :, 0].reshape(shard, inner),
        attn_total[:, :, 1].reshape(shard, inner),
        attn_total[:, :, 2].reshape(shard, inner),
        attn_total[:, :, 3].reshape(shard, inner),
        beta_grad,
        (get(OUT_RS)[:shard].astype(F32) + get((OUTSUM, 3)).astype(F32)).T,
        gate_grad,
        up_grad,
        down_grad.T,
        gains[0],
        gains[1],
    )


def solution(mesh):
    dp_size = mesh.shape["dp"]
    fine = Mesh(
        mesh.devices.reshape(dp_size // 4, 2, 2, mesh.shape["head"]), ("da", "db", "core", "head")
    )
    dp = ("da", "db", "core")
    rows = P(None, dp, "head", None)
    wide = P(dp, "head")
    tall = P("head", dp)
    in_specs = (
        rows, P(None, dp), rows, wide, wide, wide, wide, wide, tall, wide, wide, tall, P(dp), P(dp)
    )
    out_specs = (rows, rows, wide, wide, wide, wide, wide, tall, wide, wide, tall, P(dp), P(dp))
    special = dp_size == 8 and mesh.shape["head"] == 4
    return jax.shard_map(
        body if special else general_body,
        mesh=fine,
        in_specs=in_specs,
        out_specs=out_specs,
        check_vma=False,
    )
```
